32 devices in a mesh: tm: 4 (over y, x), lat: 8 (over z, core).
Axes of the slice: x: 2, y: 2, z: 4, core: 2. Of those that a mesh axis runs over, the one named last changes fastest.
Arguments:
- frames: bfloat16 [64, 2048, 4096], P('tm', 'lat'), may hold values from -6 to 6
- owner_map: int32 [512], replicated, may hold values from 0 to 511, as said below
Outputs:
- spectrum: float32 [2, 512, 8, 1024], P(None, 'lat', None, 'tm')
The draws below stay inside these ranges and needn't reach their ends.
Inputs may be any that keep to these rules, and one draw needn't show every extreme that they name: owner_map is a permutation of 0 to 511; entries 2 i and 2 i + 1 hold an order m and the order 512 - 1 - m.
All inputs are finite; a program needn't handle non-finite values.
Results may differ from the reference program's by a relative error of at most 0.0064.
Values may be sent and summed in bfloat16 or wider, within the bound.
No kernel may reach another device: no remote copies, remote signals or barrier semaphores. Data moves between devices by JAX's collectives and lax.ppermute only.
A program may use at most 128 MiB of HBM per device.

```python
import math
from functools import partial
import jax
import jax.numpy as jnp
from jax import lax

NLON = 4096
NLAT = 2048
M = 512
L = 1024
F = 8
FRAMES = 64


def draw_owner_map(key, part):
    pair_ids = jax.random.permutation(jax.random.fold_in(key, 11), M // 2).astype(jnp.int32)
    flips = jax.random.randint(jax.random.fold_in(key, 12), (M // 2,), 0, 2).astype(jnp.int32)
    leading = jnp.where(flips == 1, M - 1 - pair_ids, pair_ids)
    partner = M - 1 - leading
    return jnp.stack([leading, partner], axis=1).reshape(M).astype(jnp.int32)


def steps_of(key, extent, shards, low, high):
    gain = 1.0
    for position, parts in shards:
        heights = jax.random.uniform(jax.random.fold_in(jax.random.fold_in(key, 6), position), (parts,), jnp.float32, low / len(shards), high / len(shards))
        gain = gain * jnp.repeat(jnp.exp(heights), extent[position] // parts).reshape((-1,) + (1,) * (len(extent) - 1 - position))
    return gain


def bell_draw(stream_key, shape, deviation, limit, split=(), kind=jnp.bfloat16):
    gain = steps_of(stream_key, shape, split, -0.22, 0.18) if split else 1.0
    entries = jax.random.normal(stream_key, shape, jnp.float32) * deviation * gain
    return jnp.minimum(jnp.maximum(entries, -limit), limit).astype(kind)


def setup_inputs(seed: int = 0) -> dict:
    keys = jax.random.split(jax.random.key(seed), 3)
    frames = bell_draw(keys[0], (FRAMES, NLAT, NLON), 1.0, 6.0, ((0, 4), (1, 8)))
    owner_map = draw_owner_map(jax.random.fold_in(keys[2], 71), 0)
    return dict(frames=frames, owner_map=owner_map)


def longitude_table(owner_map, nlon_count):
    columns = owner_map.astype(jnp.int32)
    points = jnp.arange(nlon_count, dtype=jnp.int32)
    phases = points[:, None] * columns[None, :] % nlon_count
    angles = phases.astype(jnp.float32) * (2.0 * math.pi / nlon_count)
    factor = math.sqrt(2.0 / nlon_count)
    cos_part = (jnp.cos(angles) * factor).astype(jnp.bfloat16)
    sin_part = (-jnp.sin(angles) * factor).astype(jnp.bfloat16)
    return jnp.concatenate([cos_part, sin_part], axis=1)

def order_setup(orders, nlat_count, order_count):
    order_val = orders.astype(jnp.float32)[:, None]
    steps_k = jnp.arange(1, order_count + 1, dtype=jnp.float32)[None, :]
    growth = lax.optimization_barrier(jnp.sum(jnp.where(steps_k <= order_val, jnp.log1p(0.5 / steps_k), 0.0), axis=1, keepdims=True))
    colatitude = (jnp.arange(nlat_count, dtype=jnp.float32) + 0.5) * (math.pi / nlat_count)
    cosine = jnp.cos(colatitude)
    sine_row = jnp.sin(colatitude)
    lognorm = 0.5 * math.log(0.5) + 0.5 * growth + order_val * jnp.log(sine_row)[None, :]
    weight = sine_row * (math.pi / nlat_count) * math.sqrt(nlat_count)
    safe_log = jnp.maximum(lognorm, -60.0)
    start_value = jnp.where(lognorm >= -60.0, jnp.exp(safe_log), 0.0)
    diagonal_start = start_value * weight[None, :]
    return (order_val, cosine, diagonal_start)

def legendre_step(order_val, cosine, diagonal_start, state, degree):
    previous_p, older_p = state
    level = degree.astype(jnp.float32)
    level_sq = level * level
    order_sq = order_val * order_val
    lower = level - 1.0
    rising_coef = jnp.sqrt(jnp.maximum(4.0 * level_sq - 1.0, 0.0) / jnp.maximum(level_sq - order_sq, 1.0))
    falling_coef = jnp.sqrt(jnp.maximum(lower * lower - order_sq, 0.0) / jnp.maximum(4.0 * lower * lower - 1.0, 1.0))
    rising = rising_coef * (cosine[None, :] * previous_p - falling_coef * older_p)
    current = jnp.where(level == order_val, diagonal_start, jnp.where(level > order_val, rising, 0.0))
    return ((current, previous_p), current.astype(jnp.bfloat16))

def time_table(total_frames, band_count, first_frame, frame_count):
    frames_at = first_frame + jnp.arange(frame_count, dtype=jnp.int32)
    frequency = total_frames // 8 + jnp.arange(band_count, dtype=jnp.int32)
    phases = frequency[:, None] * frames_at[None, :] % total_frames
    angles = phases.astype(jnp.float32) * (2.0 * math.pi / total_frames)
    factor = 1.0 / math.sqrt(total_frames)
    cos_part = jnp.cos(angles) * factor
    sin_part = jnp.sin(angles) * factor
    top_row = jnp.stack([cos_part, sin_part], axis=1)
    low_row = jnp.stack([-sin_part, cos_part], axis=1)
    return jnp.stack([top_row, low_row], axis=0).astype(jnp.bfloat16)

def spectrum_block(band_block, orders, nlat_count, degree_count, order_count):
    order_val, cosine, diagonal_start = order_setup(orders, nlat_count, order_count)
    zero_rows = jnp.zeros(diagonal_start.shape, jnp.float32)
    stepper = partial(legendre_step, order_val, cosine, diagonal_start)
    _, polynomials = lax.scan(stepper, (zero_rows, zero_rows), jnp.arange(degree_count, dtype=jnp.int32))
    return jnp.einsum('ekfr,lkr->ekfl', band_block.astype(jnp.float32), polynomials.astype(jnp.float32))

def reference(frames, owner_map):
    lon_weights = longitude_table(owner_map, NLON).astype(jnp.float32)
    weights = time_table(FRAMES, F, 0, FRAMES).astype(jnp.float32)
    weight_cols = jnp.moveaxis(weights, 3, 0)

    def one_frame(total, packed):
        image, weight_col = packed
        coef = jnp.dot(image.astype(jnp.float32), lon_weights, precision=lax.Precision.HIGHEST).astype(jnp.bfloat16)
        coef = lax.optimization_barrier(coef).astype(jnp.float32).reshape(NLAT, 2, M)
        return (total + jnp.einsum('efc,rck->ekfr', weight_col, coef, precision=lax.Precision.HIGHEST), None)
    start_total = jnp.zeros((2, M, F, NLAT), jnp.float32)
    band, _ = lax.scan(one_frame, start_total, (frames, weight_cols))
    band = band.astype(jnp.bfloat16)
    group_size = min(32, M)
    group_count = M // group_size
    grouped = jnp.moveaxis(band.reshape(2, group_count, group_size, F, NLAT), 1, 0)
    orders = owner_map.reshape(group_count, group_size)

    def one_group(packed):
        return spectrum_block(packed[0], packed[1], NLAT, L, M)
    spectra = lax.map(one_group, (grouped, orders))
    return jnp.moveaxis(spectra, 0, 1).reshape(2, M, F, L)
```

```python
from functools import partial
import math

import jax
import jax.numpy as jnp
import numpy as np
from jax import lax
from jax.experimental import pallas as pl
from jax.experimental.pallas import tpu as pltpu
from jax.sharding import PartitionSpec as P

L = 1024
F = 8
EF = 2 * F
ROWS = 16
WIDE = ROWS * EF
CHUNKS = 4
GROUP = 8
SPAN = 128
VMEM = 48 * 1024 * 1024


def natural_tables(nlon, order_count):
    half = nlon // 2
    points = np.arange(half, dtype=np.int64)[None, :]
    factor = np.float32(math.sqrt(2.0 / nlon))
    tables = []
    for parity in range(2):
        orders = np.arange(parity, order_count, 2, dtype=np.int64)[:, None]
        angles = (orders * points % nlon).astype(np.float32) * np.float32(2.0 * math.pi / nlon)
        parts = [np.cos(angles) * factor, -np.sin(angles) * factor]
        tables.append(np.concatenate(parts, axis=0).astype(jnp.bfloat16))
    return tables


def time_table(total_frames, band_count, first_frame, frame_count):
    frames_at = first_frame + jnp.arange(frame_count, dtype=jnp.int32)
    frequency = total_frames // 8 + jnp.arange(band_count, dtype=jnp.int32)
    phases = frequency[:, None] * frames_at[None, :] % total_frames
    angles = phases.astype(jnp.float32) * (2.0 * math.pi / total_frames)
    factor = 1.0 / math.sqrt(total_frames)
    cos_part = jnp.cos(angles) * factor
    sin_part = jnp.sin(angles) * factor
    top_row = jnp.stack([cos_part, sin_part], axis=1)
    low_row = jnp.stack([-sin_part, cos_part], axis=1)
    return jnp.stack([top_row, low_row], axis=0).astype(jnp.bfloat16)


def transform_kernel(south_ref, frames_ref, even_ref, odd_ref, time_ref, place_ref, *outs):
    frame_count, rows, nlon = frames_ref.shape
    half = nlon // 2
    image = frames_ref[...].reshape(frame_count * rows, nlon)
    near, far = image[:, :half], image[:, half:]
    bands = []
    for table_ref, folded in ((even_ref, near + far), (odd_ref, near - far)):
        count = table_ref.shape[0] // 2
        coef = lax.dot_general(
            table_ref[...], folded, (((1,), (1,)), ((), ())), preferred_element_type=jnp.float32
        ).astype(jnp.bfloat16)
        bands.append(
            jnp.dot(coef[:count], time_ref[0], preferred_element_type=jnp.float32)
            + jnp.dot(coef[count:], time_ref[1], preferred_element_type=jnp.float32)
        )
    band = jnp.concatenate(bands, axis=0).astype(jnp.bfloat16)
    placed = jnp.dot(place_ref[...], band, preferred_element_type=jnp.float32).astype(jnp.bfloat16)
    size = outs[0].shape[0]
    for i, out in enumerate(outs):
        out[...] = placed[i * size : (i + 1) * size]


def transform_chunk(chunk, south, frames, even, odd, time_mat, place):
    frame_count, row_count, nlon = frames.shape
    blocks = row_count // ROWS
    per_chunk = blocks // CHUNKS
    order_count = place.shape[0]
    size = order_count // 4

    def frame_block(b, south_ref):
        at = chunk * per_chunk + b
        return (0, jnp.where(south_ref[0] == 1, blocks - 1 - at, at), 0)

    def whole(b, south_ref):
        return (0, 0)

    out = jax.ShapeDtypeStruct((size, per_chunk * WIDE), jnp.bfloat16)
    flops = 2 * blocks // CHUNKS * WIDE * order_count * (nlon + 2 * WIDE + order_count)
    return pl.pallas_call(
        transform_kernel,
        grid_spec=pltpu.PrefetchScalarGridSpec(
            num_scalar_prefetch=1,
            grid=(per_chunk,),
            in_specs=[
                pl.BlockSpec((frame_count, ROWS, nlon), frame_block),
                pl.BlockSpec(even.shape, whole),
                pl.BlockSpec(odd.shape, whole),
                pl.BlockSpec(time_mat.shape, lambda b, s: (0, 0, 0)),
                pl.BlockSpec(place.shape, whole),
            ],
            out_specs=[pl.BlockSpec((size, WIDE), lambda b, s: (0, b))] * 4,
        ),
        out_shape=[out] * 4,
        compiler_params=pltpu.CompilerParams(vmem_limit_bytes=VMEM),
        cost_estimate=pl.CostEstimate(
            flops=flops, bytes_accessed=frames.size * 2 // CHUNKS + 4 * 2**20, transcendentals=0
        ),
        name="longitude_time",
    )(south, frames, even, odd, time_mat, place)


def degree_tables(orders, degree_count):
    level = jnp.arange(degree_count, dtype=jnp.float32)[None, :]
    level_sq = level * level
    order_sq = jnp.square(orders.astype(jnp.float32))[:, None]
    lower = level - 1.0
    rising = jnp.sqrt(
        jnp.maximum(4.0 * level_sq - 1.0, 0.0) / jnp.maximum(level_sq - order_sq, 1.0)
    )
    falling = jnp.sqrt(
        jnp.maximum(lower * lower - order_sq, 0.0) / jnp.maximum(4.0 * lower * lower - 1.0, 1.0)
    )
    return rising, rising * falling


def order_start(orders, rows, nlat_count, order_count):
    order_val = orders.astype(jnp.float32)[:, None]
    steps_k = jnp.arange(1, order_count + 1, dtype=jnp.float32)[None, :]
    growth = jnp.sum(
        jnp.where(steps_k <= order_val, jnp.log1p(0.5 / steps_k), 0.0), axis=1, keepdims=True
    )
    colatitude = (rows.astype(jnp.float32) + 0.5) * (math.pi / nlat_count)
    cosine = jnp.cos(colatitude)
    sine_row = jnp.sin(colatitude)
    lognorm = 0.5 * math.log(0.5) + 0.5 * growth + order_val * jnp.log(sine_row)[None, :]
    weight = sine_row * (math.pi / nlat_count) * math.sqrt(nlat_count)
    safe_log = jnp.maximum(lognorm, -60.0)
    start_value = jnp.where(lognorm >= -60.0, jnp.exp(safe_log), 0.0)
    return cosine, start_value * weight[None, :]


def polynomial_kernel(
    half,
    order_ref, rise_a, fall_a, rise_b, fall_b, x_ref, start_a, start_b,
    out_a, out_b, state_a, state_b,
):
    step = pl.program_id(0)
    base = step * SPAN
    chunks, _, lanes_a = out_a.shape
    lanes_b = out_b.shape[2]

    @pl.when(step == 0)
    def _():
        state_a[...] = jnp.zeros_like(state_a)
        state_b[...] = jnp.zeros_like(state_b)

    x_a = x_ref[...]
    x_b = jnp.concatenate(
        [x_a[:, (c + 1) * lanes_a - lanes_b : (c + 1) * lanes_a] for c in range(chunks)], axis=1
    )
    group_a = (0, rise_a, fall_a, x_a, start_a, state_a, out_a, lanes_a)
    group_b = (1, rise_b, fall_b, x_b, start_b, state_b, out_b, lanes_b)

    def run(*groups):
        states = [(g[5][0], g[5][1]) for g, _ in groups]
        for i in range(SPAN // 2):
            for n, ((which, rise, fall, x, start, _, out, lanes), begins) in enumerate(groups):
                made = []
                for at in (2 * i, 2 * i + 1):
                    older, last = states[n]
                    new = (rise[:, at : at + 1] * x) * last - fall[:, at : at + 1] * older
                    if begins:
                        here = jnp.where(order_ref[which, :, :1] == base + at, 1.0, 0.0)
                        new = new + here * start[...]
                    states[n] = (last, new)
                    made.append(new)
                both = jnp.concatenate(made, axis=0).astype(jnp.bfloat16)
                for c in range(chunks):
                    out[c, 2 * GROUP * i : 2 * GROUP * (i + 1), :] = both[
                        :, c * lanes : (c + 1) * lanes
                    ]
        for (g, _), state in zip(groups, states):
            g[5][0], g[5][1] = state

    @pl.when(step < half)
    def _():
        run((group_a, True))

    @pl.when(jnp.logical_and(step >= half, step < 2 * half))
    def _():
        run((group_a, False), (group_b, True))

    @pl.when(step >= 2 * half)
    def _():
        run((group_a, False), (group_b, False))


def polynomials(small, large, order_count, nlat, rows_each):
    nlat_count = nlat * rows_each
    half = order_count // 2 // SPAN
    rows = jnp.arange(nlat_count // 2, dtype=jnp.int32)
    rows = rows.reshape(nlat // 2, CHUNKS, rows_each // CHUNKS).transpose(1, 0, 2)
    lanes_a = nlat_count // 2 // CHUNKS
    lanes_b = lanes_a // 2
    cosine, start_a = order_start(small, rows.reshape(-1), nlat_count, order_count)
    _, start_b = order_start(
        large, rows[:, nlat // 4 :].reshape(-1), nlat_count, order_count
    )
    rise_a, fall_a = degree_tables(small, L)
    rise_b, fall_b = degree_tables(large, L)
    orders = jnp.broadcast_to(jnp.stack([small, large])[:, :, None], (2, GROUP, 128))
    x = jnp.broadcast_to(cosine[None, :], (GROUP, nlat_count // 2))
    table = pl.BlockSpec((GROUP, SPAN), lambda s: (0, s))

    def fixed(shape):
        return pl.BlockSpec(shape, lambda s: (0,) * len(shape))

    return pl.pallas_call(
        partial(polynomial_kernel, half),
        grid=(L // SPAN,),
        in_specs=[
            fixed(orders.shape), table, table, table, table,
            fixed(x.shape), fixed(start_a.shape), fixed(start_b.shape),
        ],
        out_specs=[
            pl.BlockSpec((CHUNKS, SPAN * GROUP, lanes_a), lambda s: (0, s, 0)),
            pl.BlockSpec(
                (CHUNKS, SPAN * GROUP, lanes_b), lambda s: (0, jnp.maximum(s - half, 0), 0)
            ),
        ],
        out_shape=[
            jax.ShapeDtypeStruct((CHUNKS, L * GROUP, lanes_a), jnp.bfloat16),
            jax.ShapeDtypeStruct(
                (CHUNKS, (L - order_count // 2) * GROUP, lanes_b), jnp.bfloat16
            ),
        ],
        scratch_shapes=[
            pltpu.VMEM((2,) + start_a.shape, jnp.float32),
            pltpu.VMEM((2,) + start_b.shape, jnp.float32),
        ],
        compiler_params=pltpu.CompilerParams(vmem_limit_bytes=VMEM),
        cost_estimate=pl.CostEstimate(
            flops=2 * 10**9, bytes_accessed=24 * 2**20, transcendentals=0
        ),
        name="legendre",
    )(orders, rise_a, fall_a, rise_b, fall_b, x, start_a, start_b)


def swap_groups(x):
    sub = lax.broadcasted_iota(jnp.int32, x.shape, 1)
    lane = lax.broadcasted_iota(jnp.int32, x.shape, 2) // EF
    for bit in (1, 2, 4):
        down = pltpu.roll(pltpu.roll(x, 8 - bit, 1), EF * bit, 2)
        up = pltpu.roll(pltpu.roll(x, bit, 1), 128 - EF * bit, 2)
        sub_on, lane_on = (sub & bit) != 0, (lane & bit) != 0
        x = jnp.where(sub_on == lane_on, x, jnp.where(sub_on, up, down))
    return x


def contract_kernel(half, last, z_ref, mask_ref, p_a, p_b, *refs):
    acc_ref = refs[0] if len(refs) == 4 else None
    out_ref, w_a, w_b = refs[-3:]
    step = pl.program_id(0)
    nlat = z_ref.shape[0]
    lanes = z_ref.shape[2]

    @pl.when(step == 0)
    def _():
        for g, w_ref, first in ((0, w_a, 0), (1, w_b, nlat // 4)):
            for part, sign in ((0, 1.0), (1, -1.0)):
                pieces = []
                for s in range(first, nlat // 2):
                    north = z_ref[s].astype(jnp.float32)[g * GROUP : (g + 1) * GROUP]
                    south = z_ref[nlat - 1 - s].astype(jnp.float32)[g * GROUP : (g + 1) * GROUP]
                    both = north + sign * south
                    pieces += [both[:, i : i + 128] for i in range(0, lanes, 128)]
                block = swap_groups(jnp.stack(pieces, axis=0))
                w_ref[:, part * 128 : (part + 1) * 128] = block.reshape(
                    len(pieces) * GROUP, 128
                ).astype(jnp.bfloat16)

    def picked(p_ref, w_ref, g):
        tile = 256
        out = []
        for i in range(0, SPAN * GROUP, tile):
            product = jnp.dot(
                p_ref[0, i : i + tile, :], w_ref[...], preferred_element_type=jnp.float32
            ).reshape(tile // 16, 16, 256)
            kept = product[:, :, :128] * mask_ref[g, 0] + product[:, :, 128:] * mask_ref[g, 1]
            out.append(jnp.sum(kept.reshape(tile // GROUP, GROUP, 128), axis=1))
        return jnp.concatenate(out, axis=0)

    def put(part, value):
        at = slice(part * 128, (part + 1) * 128)
        if acc_ref is not None:
            value = value + acc_ref[:, at]
        if last:
            out_ref[0, at, :] = value.T.astype(out_ref.dtype)
        else:
            out_ref[:, at] = value

    put(0, picked(p_a, w_a, 0))

    @pl.when(step < half)
    def _():
        put(1, jnp.zeros((SPAN, 128), jnp.float32))

    @pl.when(step >= half)
    def _():
        put(1, picked(p_b, w_b, 1))


def contract_chunk(chunk, z, masks, p_a, p_b, acc, half, ntm):
    last = chunk == CHUNKS - 1
    lanes_a, lanes_b = p_a.shape[2], p_b.shape[2]
    acc_spec = pl.BlockSpec((SPAN, 256), lambda s: (s, 0))
    spans = L // ntm // SPAN
    if last:
        out_shape = jax.ShapeDtypeStruct((ntm, 256, L // ntm), jnp.bfloat16)
        out_spec = pl.BlockSpec((1, 256, SPAN), lambda s: (s // spans, 0, s % spans))
    else:
        out_shape = jax.ShapeDtypeStruct((L, 256), jnp.float32)
        out_spec = acc_spec
    return pl.pallas_call(
        partial(contract_kernel, half, last),
        grid=(L // SPAN,),
        in_specs=[
            pl.BlockSpec(z.shape, lambda s: (0, 0, 0)),
            pl.BlockSpec(masks.shape, lambda s: (0, 0, 0, 0)),
            pl.BlockSpec((1, SPAN * GROUP, lanes_a), lambda s: (chunk, s, 0)),
            pl.BlockSpec(
                (1, SPAN * GROUP, lanes_b), lambda s: (chunk, jnp.maximum(s - half, 0), 0)
            ),
        ]
        + [acc_spec] * (acc is not None),
        out_specs=out_spec,
        out_shape=out_shape,
        scratch_shapes=[
            pltpu.VMEM((lanes_a, 256), jnp.bfloat16),
            pltpu.VMEM((lanes_b, 256), jnp.bfloat16),
        ],
        compiler_params=pltpu.CompilerParams(vmem_limit_bytes=VMEM),
        cost_estimate=pl.CostEstimate(
            flops=2 * L * GROUP * (lanes_a + lanes_b) * 256,
            bytes_accessed=L * GROUP * (lanes_a + lanes_b) * 2 + 2 * 2**20,
            transcendentals=0,
        ),
        name="latitude_sum",
    )(z, masks, p_a, p_b, *([acc] if acc is not None else []))


def swap_with(x, axis, bit):
    count = lax.axis_size(axis)
    return lax.ppermute(x, axis, [(i, i ^ (1 << bit)) for i in range(count)])


def add(a, b):
    return (a.astype(jnp.float32) + b.astype(jnp.float32)).astype(jnp.bfloat16)


def reduce_over_time(keep, send, bits):
    for i, bit in enumerate(bits):
        got = swap_with(send, "tm", bit)
        if i == len(bits) - 1:
            return add(keep, got)
        middle = keep.shape[0] // 2
        send = add(keep[middle:], got[middle:])
        keep = add(keep[:middle], got[:middle])


def bit_order(bits, count):
    offsets = []
    for position in range(count):
        offset = 0
        for i, bit in enumerate(bits):
            if position >> (len(bits) - 1 - i) & 1:
                offset |= 1 << bit
        offsets.append(offset)
    return jnp.array(offsets, jnp.int32)


def shards(frames, owner_map):
    frame_count, row_count, nlon = frames.shape
    order_count = owner_map.shape[0]
    nlat, ntm = lax.axis_size("lat"), lax.axis_size("tm")
    my_tm, my_lat = lax.axis_index("tm"), lax.axis_index("lat")
    south = my_lat >= nlat // 2
    levels = ntm.bit_length() - 1
    bits_a = list(range(levels))
    bits_b = bits_a[-1:] + bits_a[:-1]

    pairs = owner_map.reshape(nlat, ntm, -1, 2)
    owned = pairs.shape[2]
    small, large = jnp.min(pairs, axis=3), jnp.max(pairs, axis=3)

    def in_order(orders, bits):
        return orders.transpose(1, 0, 2)[bit_order(bits, ntm) ^ my_tm].reshape(-1)

    wanted = jnp.concatenate([in_order(small, bits_a), in_order(large, bits_b)])
    wanted = wanted // 2 + wanted % 2 * (order_count // 2)
    place = (wanted[:, None] == jnp.arange(order_count, dtype=jnp.int32)[None, :]).astype(
        jnp.bfloat16
    )
    even, odd = (jnp.asarray(t) for t in natural_tables(nlon, order_count))
    weights = time_table(frame_count * ntm, F, my_tm * frame_count, frame_count)
    row_in, row_out = jnp.arange(ROWS)[:, None], jnp.arange(ROWS)[None, :]
    same_row = (jnp.where(south, ROWS - 1 - row_in, row_in) == row_out).astype(jnp.bfloat16)
    time_mat = (
        weights.transpose(2, 3, 0, 1).reshape(2, frame_count, 1, 1, EF)
        * same_row[None, None, :, :, None]
    ).reshape(2, frame_count * ROWS, WIDE)
    south_flag = south.astype(jnp.int32).reshape(1)

    def padded(orders):
        return jnp.pad(orders[my_lat, my_tm], (0, GROUP - owned), mode="edge")

    my_small, my_large = padded(small), padded(large)
    p_a, p_b = polynomials(my_small, my_large, order_count, nlat, row_count)
    half = order_count // 2 // SPAN
    mine = jnp.stack([my_small, my_large])
    slot = jnp.arange(GROUP)
    own = slot[:, None] == (jnp.arange(128) // EF)[None, :]
    parity = (mine[:, None, :] + jnp.arange(2)[None, :, None]) % 2
    masks = jnp.stack(
        [
            (own[None, None] & (parity[..., None] == u)).reshape(2, 2 * GROUP, 128)
            for u in range(2)
        ],
        axis=1,
    ).astype(jnp.float32)

    acc = None
    for chunk in range(CHUNKS):
        keep_a, send_a, keep_b, send_b = transform_chunk(
            chunk, south_flag, frames, even, odd, time_mat, place
        )
        done_a = reduce_over_time(keep_a, send_a, bits_a)
        done_b = reduce_over_time(keep_b, send_b, bits_b)
        width = done_a.shape[1]
        band = jnp.concatenate(
            [done_a.reshape(nlat, owned, width), done_b.reshape(nlat, owned, width)], axis=1
        )
        band = lax.all_to_all(band, "lat", split_axis=0, concat_axis=0, tiled=True)
        if owned < GROUP:
            band = jnp.pad(
                band.reshape(nlat, 2, owned, width),
                ((0, 0), (0, 0), (0, GROUP - owned), (0, 0)),
            ).reshape(nlat, 2 * GROUP, width)
        acc = contract_chunk(chunk, band, masks, p_a, p_b, acc, half, ntm)

    spectra = lax.all_to_all(acc, "tm", split_axis=0, concat_axis=0, tiled=True)
    spectra = spectra.reshape(ntm, 2, GROUP, 2, F, L // ntm)[:, :, :owned]
    first_small = (pairs[my_lat, :, :, 0] < order_count // 2)[:, :, None, None, None]
    low, high = spectra[:, 0], spectra[:, 1]
    slots = jnp.stack(
        [jnp.where(first_small, low, high), jnp.where(first_small, high, low)], axis=2
    )
    slots = slots.transpose(3, 0, 1, 2, 4, 5).reshape(2, ntm * owned * 2, F, L // ntm)
    return slots.astype(jnp.float32)


def solution(mesh):
    return jax.shard_map(
        shards,
        mesh=mesh,
        in_specs=(P("tm", "lat", None), P()),
        out_specs=P(None, "lat", None, "tm"),
        check_vma=False,
    )
```

```python
from functools import partial
import math

import jax
import jax.numpy as jnp
import numpy as np
from jax import lax
from jax.experimental import pallas as pl
from jax.experimental.pallas import tpu as pltpu
from jax.sharding import PartitionSpec as P

L = 1024
F = 8
EF = 2 * F
ROWS = 16
WIDE = ROWS * EF
QUARTERS = (2, 2)
GROUP = 8
SPAN = 128
SPAN_OUT = 256
VMEM = 24 * 1024 * 1024
VMEM_LEGENDRE = 8 * 1024 * 1024
VMEM_SUM = 24 * 1024 * 1024


def longitude_tables(nlon, order_count):
    factor = np.float32(math.sqrt(2.0 / nlon))
    tables = []
    for first, stride, length in ((0, 4, nlon // 4), (2, 4, nlon // 4), (1, 2, nlon // 2)):
        points = np.arange(length, dtype=np.int64)[:, None]
        orders = np.arange(first, order_count, stride, dtype=np.int64)[None, :]
        angles = (orders * points % nlon).astype(np.float32) * np.float32(2.0 * math.pi / nlon)
        parts = [np.cos(angles) * factor, -np.sin(angles) * factor]
        tables.append(np.concatenate(parts, axis=1).astype(jnp.bfloat16))
    return tables


def table_column(orders, order_count):
    quarter = orders // 4 + orders % 4 // 2 * (order_count // 4)
    return jnp.where(orders % 2 == 1, order_count // 2 + orders // 2, quarter)


def time_matrices(frame_count, time_count):
    total = frame_count * time_count
    frames_at = np.arange(total, dtype=np.int64)
    frequency = total // 8 + np.arange(F, dtype=np.int64)
    phases = frequency[:, None] * frames_at[None, :] % total
    angles = phases.astype(np.float32) * np.float32(2.0 * math.pi / total)
    factor = np.float32(1.0 / math.sqrt(total))
    cos_part, sin_part = np.cos(angles) * factor, np.sin(angles) * factor
    weights = np.stack(
        [np.concatenate([cos_part, -sin_part]), np.concatenate([sin_part, cos_part])]
    )
    weights = weights.reshape(2, EF, time_count, frame_count).transpose(2, 0, 1, 3)
    same = np.stack([np.eye(ROWS), np.eye(ROWS)[::-1]]).astype(np.float32)
    full = weights[:, None, :, None, :, :, None] * same[None, :, None, :, None, None, :]
    return full.reshape(time_count, 2, 2, WIDE, frame_count * ROWS).astype(jnp.bfloat16)


SHORT = pl.CostEstimate(flops=10**6, bytes_accessed=10**5, transcendentals=0)


def product(a, b):
    return jnp.dot(a, b, preferred_element_type=jnp.float32)


def transform_kernel(where_ref, frames_ref, fours_ref, twos_ref, odd_ref, time_ref, place_ref, *refs):
    frame_count, rows, nlon = frames_ref.shape
    outs, (sum_s, diff_s, odd_s) = refs[:4], refs[4:]
    half, quarter = nlon // 2, nlon // 4
    count = rows // ROWS
    tall = frame_count * ROWS
    for i in range(count):
        at = slice(i * tall, (i + 1) * tall)
        first = jnp.where(where_ref[0] == 1, count - 1 - i, i) * ROWS
        image = frames_ref[:, pl.ds(pl.multiple_of(first, ROWS), ROWS), :].reshape(tall, nlon)
        near, far = image[:, :half], image[:, half:]
        even = near + far
        odd_s[at] = near - far
        sum_s[at] = even[:, :quarter] + even[:, quarter:]
        diff_s[at] = even[:, :quarter] - even[:, quarter:]
    coefs = [
        product(folded[...], table_ref[...]).astype(jnp.bfloat16)
        for folded, table_ref in ((sum_s, fours_ref), (diff_s, twos_ref), (odd_s, odd_ref))
    ]
    for i in range(count):
        bands = []
        for coef in coefs:
            coef = coef[i * tall : (i + 1) * tall]
            middle = coef.shape[1] // 2
            bands.append(
                product(time_ref[0, 0, 0], coef[:, :middle])
                + product(time_ref[0, 0, 1], coef[:, middle:])
            )
        band = jnp.concatenate(bands, axis=1).astype(jnp.bfloat16)
        placed = lax.dot_general(
            place_ref[...], band, (((1,), (1,)), ((), ())), preferred_element_type=jnp.float32
        ).astype(jnp.bfloat16)
        size = outs[0].shape[0]
        for n, out in enumerate(outs):
            out[:, i * WIDE : (i + 1) * WIDE] = placed[n * size : (n + 1) * size]


def transform_chunk(part, where, frames, tables, time_mats, place):
    frame_count, row_count, nlon = frames.shape
    first, blocks = part
    together = 2 if first % 2 == 0 and blocks % 2 == 0 else 1
    rows = together * ROWS
    steps, first, all_steps = blocks // together, first // together, row_count // rows
    order_count = place.shape[0]
    size = order_count // 4

    def frame_block(b, where_ref):
        at = first + b
        return (0, jnp.where(where_ref[0] == 1, all_steps - 1 - at, at), 0)

    def time_block(b, where_ref):
        return (where_ref[1], where_ref[0], 0, 0, 0)

    out = pltpu.HBM((size, blocks * WIDE), jnp.bfloat16)
    tall = frame_count * rows
    flops = 2 * steps * tall * order_count * (3 * nlon // 4 + 2 * WIDE + order_count)
    in_vmem = pl.BlockSpec(memory_space=pltpu.VMEM)
    return pl.pallas_call(
        transform_kernel,
        grid_spec=pltpu.PrefetchScalarGridSpec(
            num_scalar_prefetch=1,
            grid=(steps,),
            in_specs=[
                pl.BlockSpec((frame_count, rows, nlon), frame_block),
                *([in_vmem] * len(tables)),
                pl.BlockSpec((1, 1) + time_mats.shape[2:], time_block),
                in_vmem,
            ],
            out_specs=[pl.BlockSpec((size, rows * EF), lambda b, w: (0, b))] * 4,
            scratch_shapes=[
                pltpu.VMEM((tall, nlon // 4), jnp.bfloat16),
                pltpu.VMEM((tall, nlon // 4), jnp.bfloat16),
                pltpu.VMEM((tall, nlon // 2), jnp.bfloat16),
            ],
        ),
        out_shape=[out] * 4,
        compiler_params=pltpu.CompilerParams(vmem_limit_bytes=VMEM),
        cost_estimate=SHORT,
        name="longitude_time",
    )(where, frames, *tables, pltpu.with_memory_space_constraint(time_mats, pltpu.HBM), place)


def degree_factors(orders, level):
    level_sq = level * level
    order_sq = orders * orders
    lower = level - 1.0
    rising = jnp.sqrt(
        jnp.maximum(4.0 * level_sq - 1.0, 0.0) / jnp.maximum(level_sq - order_sq, 1.0)
    )
    falling = jnp.sqrt(
        jnp.maximum(lower * lower - order_sq, 0.0) / jnp.maximum(4.0 * lower * lower - 1.0, 1.0)
    )
    return rising, rising * falling


def polynomial_kernel(half, begin, orders_ref, growth_ref, rows_ref, out, token, state):
    step = pl.program_id(0)
    base = begin + step * SPAN
    order_count = growth_ref.shape[1]

    def spread(row):
        return jnp.broadcast_to(row, (GROUP, row.shape[1]))

    @pl.when(step == 0)
    def _():
        steps_k = lax.broadcasted_iota(jnp.int32, (GROUP, order_count), 1).astype(jnp.float32) + 1.0
        order = orders_ref[:, :1]
        growth = jnp.sum(
            jnp.where(steps_k <= order, spread(growth_ref[...]), 0.0), axis=1, keepdims=True
        )
        lognorm = 0.5 * math.log(0.5) + 0.5 * growth + order * spread(rows_ref[1:2])
        start = jnp.where(lognorm >= -60.0, jnp.exp(jnp.maximum(lognorm, -60.0)), 0.0)
        token[...] = jnp.zeros_like(token)
        state[0] = jnp.zeros_like(start)
        state[1] = jnp.zeros_like(start)
        state[2] = start * spread(rows_ref[2:3])

    x = spread(rows_ref[0:1])

    def run(begins):
        level = (lax.broadcasted_iota(jnp.int32, (GROUP, SPAN), 1) + base).astype(jnp.float32)
        rise, fall = degree_factors(orders_ref[...], level)
        older, last = state[0], state[1]
        first = pl.multiple_of(step * SPAN * GROUP, SPAN * GROUP)
        for at in range(0, SPAN, 2):
            made = []
            for i in (at, at + 1):
                new = (rise[:, i : i + 1] * x) * last - fall[:, i : i + 1] * older
                if begins:
                    here = jnp.where(orders_ref[...] == (base + i).astype(jnp.float32), 1.0, 0.0)
                    new = new + here[:, :1] * state[2]
                older, last = last, new
                made.append(new)
            both = jnp.concatenate(made, axis=0).astype(jnp.bfloat16)
            out[pl.ds(first + GROUP * at, 2 * GROUP), :] = both
        state[0], state[1] = older, last

    @pl.when(step < half)
    def _():
        run(True)

    @pl.when(step >= half)
    def _():
        run(False)


def polynomials(orders, which, order_count, nlat, rows_each, parts):
    nlat_count = nlat * rows_each
    half = order_count // 2 // SPAN
    rows = np.arange(nlat_count // 2).reshape(nlat // 2, rows_each)[which * nlat // 4 :]
    rows = np.concatenate(
        [rows[:, at * ROWS : (at + count) * ROWS].reshape(-1) for at, count in parts]
    )
    begin = which * order_count // 2
    colatitude = (rows.astype(np.float32) + np.float32(0.5)) * np.float32(math.pi / nlat_count)
    sine = np.sin(colatitude)
    weight = sine * np.float32(math.pi / nlat_count) * np.float32(math.sqrt(nlat_count))
    row_values = np.stack([np.cos(colatitude), np.log(sine), weight])
    growth = np.log1p(np.float32(0.5) / np.arange(1, order_count + 1, dtype=np.float32))[None, :]
    orders = jnp.broadcast_to(orders.astype(jnp.float32)[:, None], (GROUP, 128))

    def fixed(shape):
        return pl.BlockSpec(shape, lambda s: (0,) * len(shape))

    return pl.pallas_call(
        partial(polynomial_kernel, half, begin),
        grid=((L - begin) // SPAN,),
        in_specs=[fixed(orders.shape), fixed(growth.shape), fixed(row_values.shape)],
        out_specs=[pl.BlockSpec(memory_space=pltpu.VMEM), fixed((GROUP, 128))],
        out_shape=[
            jax.ShapeDtypeStruct(((L - begin) * GROUP, rows.size), jnp.bfloat16),
            jax.ShapeDtypeStruct((GROUP, 128), jnp.float32),
        ],
        scratch_shapes=[pltpu.VMEM((3, GROUP, rows.size), jnp.float32)],
        compiler_params=pltpu.CompilerParams(vmem_limit_bytes=VMEM_LEGENDRE),
        cost_estimate=SHORT,
        name="legendre",
    )(orders, jnp.asarray(growth), jnp.asarray(row_values))


def swap_groups(x):
    sub = lax.broadcasted_iota(jnp.int32, x.shape, 1)
    lane = lax.broadcasted_iota(jnp.int32, x.shape, 2) // EF
    for bit in (1, 2, 4):
        down = pltpu.roll(pltpu.roll(x, 8 - bit, 1), EF * bit, 2)
        up = pltpu.roll(pltpu.roll(x, bit, 1), 128 - EF * bit, 2)
        sub_on, lane_on = (sub & bit) != 0, (lane & bit) != 0
        x = jnp.where(sub_on == lane_on, x, jnp.where(sub_on, up, down))
    return x


def contract_kernel(g, half, last, nlat, lanes_at, here_ref, *refs):
    z_refs, (parity_ref, p_ref), refs = refs[:nlat], refs[nlat : nlat + 2], refs[nlat + 2 :]
    acc_ref = refs[0] if len(refs) == 4 else None
    out_ref, z_all, w_ref = refs[-3:]
    step = pl.program_id(0)
    lanes = z_all.shape[2]
    span = out_ref.shape[-1] if last else out_ref.shape[0]

    @pl.when(step == 0)
    def _():
        for n, z_ref in enumerate(z_refs):
            z_all[n] = z_ref[...]

        def source(s):
            return z_all[s ^ here_ref[0]].astype(jnp.float32)[g * GROUP : (g + 1) * GROUP]

        for part, sign in ((0, 1.0), (1, -1.0)):
            pieces = []
            for s in range(g * nlat // 4, nlat // 2):
                both = source(s) + sign * source(nlat - 1 - s)
                pieces += [both[:, i : i + 128] for i in range(0, lanes, 128)]
            block = swap_groups(jnp.stack(pieces, axis=0))
            w_ref[:, part * 128 : (part + 1) * 128] = block.reshape(
                len(pieces) * GROUP, 128
            ).astype(jnp.bfloat16)

    sub = lax.broadcasted_iota(jnp.int32, (GROUP, 128), 0)
    lane = lax.broadcasted_iota(jnp.int32, (GROUP, 128), 1) // EF
    odd = [((parity_ref[...] + u) & 1) == 1 for u in range(2)]

    def own_columns(first):
        tile = 4 * GROUP * GROUP
        out = []
        for i in range(0, span * GROUP, tile):
            rows = p_ref[pl.ds(first + i, tile), lanes_at : lanes_at + w_ref.shape[0]]
            full = product(rows, w_ref[...]).reshape(4, GROUP, GROUP, 256)
            kept = None
            for n in range(GROUP):
                one = jnp.where(odd[n % 2], full[:, n, :, 128:], full[:, n, :, :128])
                if n == 0:
                    kept = one
                else:
                    kept = jnp.where(((sub - lane) & 7) == n, pltpu.roll(one, n, 1), kept)
            for bit in (1, 2, 4):
                kept = jnp.where((lane & bit) != 0, pltpu.roll(kept, GROUP - bit, 1), kept)
            out.append(kept.reshape(4 * GROUP, 128))
        return jnp.concatenate(out, axis=0)

    def run():
        value = own_columns(pl.multiple_of((step - half) * span * GROUP, 256))
        if acc_ref is not None:
            value = value + acc_ref[...]
        if last:
            out_ref[0] = value.T.astype(out_ref.dtype)
        else:
            out_ref[...] = value

    if half:

        @pl.when(step < half)
        def _():
            out_ref[...] = jnp.zeros_like(out_ref)

        pl.when(step >= half)(run)
    else:
        run()


def contract_chunk(g, last, here, z, parity, p, lanes_at, lanes, acc, begin, ntm):
    each = L // ntm
    span = min(SPAN_OUT, each)
    half = begin // span if last else 0
    if last:
        steps = L // span
        per = each // span
        out_shape = jax.ShapeDtypeStruct((ntm, 128, each), jnp.bfloat16)
        out_spec = pl.BlockSpec(
            (1, 128, span), lambda s, here_ref: ((s // per) ^ here_ref[1], 0, s % per)
        )
    else:
        steps = (L - begin) // span
        out_shape = jax.ShapeDtypeStruct((L - begin, 128), jnp.float32)
        out_spec = pl.BlockSpec((span, 128), lambda s, _: (s, 0))
    acc_spec = pl.BlockSpec((span, 128), lambda s, _: (jnp.maximum(s - half, 0), 0))
    return pl.pallas_call(
        partial(contract_kernel, g, half, last, len(z), lanes_at),
        grid_spec=pltpu.PrefetchScalarGridSpec(
            num_scalar_prefetch=1,
            grid=(steps,),
            in_specs=[pl.BlockSpec(x.shape, lambda s, _: (0, 0)) for x in z]
            + [pl.BlockSpec(parity.shape, lambda s, _: (0, 0))]
            + [pl.BlockSpec(memory_space=pltpu.VMEM)]
            + [acc_spec] * (acc is not None),
            out_specs=out_spec,
            scratch_shapes=[
                pltpu.VMEM((len(z),) + z[0].shape, jnp.bfloat16),
                pltpu.VMEM((lanes, 256), jnp.bfloat16),
            ],
        ),
        out_shape=out_shape,
        compiler_params=pltpu.CompilerParams(vmem_limit_bytes=VMEM_SUM),
        cost_estimate=SHORT,
        name="latitude_sum",
    )(here, *z, parity, p, *([acc] if acc is not None else []))


def arrange_kernel(owned, here_ref, orders_ref, *refs):
    out_ref = refs[-1]
    count = (len(refs) - 1) // 2
    for offset in range(count):
        source = offset ^ here_ref[1]
        low, high = (refs[g * count + offset][...].astype(jnp.float32) for g in range(2))
        for i in range(owned):
            first = orders_ref[((here_ref[0] * count + source) * owned + i) * 2]
            in_order = first < orders_ref.shape[0] // 2
            for e in range(2):
                a, b = low[i * EF + e * F :][:F], high[i * EF + e * F :][:F]
                slot = (source * owned + i) * 2
                out_ref[e, slot] = jnp.where(in_order, a, b)
                out_ref[e, slot + 1] = jnp.where(in_order, b, a)


def arrange(here, owner_map, low, high, owned):
    ntm, each = len(low), low[0].shape[1]
    return pl.pallas_call(
        partial(arrange_kernel, owned),
        grid_spec=pltpu.PrefetchScalarGridSpec(
            num_scalar_prefetch=2,
            grid=(1,),
            in_specs=[pl.BlockSpec((128, each), lambda s, h, f: (0, 0))] * (2 * ntm),
            out_specs=pl.BlockSpec((2, ntm * owned * 2, F, each), lambda s, h, f: (0, 0, 0, 0)),
        ),
        out_shape=jax.ShapeDtypeStruct((2, ntm * owned * 2, F, each), jnp.float32),
        name="slot_order",
    )(here, owner_map, *low, *high)


def swap_with(x, axis, offset):
    count = lax.axis_size(axis)
    return lax.ppermute(x, axis, [(i, i ^ offset) for i in range(count)])


def both_sums(keep_a, got_a, keep_b, got_b):
    return [
        k[...].astype(jnp.float32) + g[...].astype(jnp.float32)
        for k, g in ((keep_a, got_a), (keep_b, got_b))
    ]


def halve_kernel(keep_a, got_a, keep_b, got_b, *outs):
    outs = outs[-4:]
    for n, total in enumerate(both_sums(keep_a, got_a, keep_b, got_b)):
        middle = total.shape[0] // 2
        outs[2 * n][...] = total[:middle]
        outs[2 * n + 1][...] = total[middle:].astype(jnp.bfloat16)


def finish_kernel(keep_a, got_a, keep_b, got_b, *outs):
    total_a, total_b = both_sums(keep_a, got_a, keep_b, got_b)
    owned = total_a.shape[0] // len(outs)
    for n, out in enumerate(outs):
        at = slice(n * owned, (n + 1) * owned)
        out[...] = jnp.concatenate([total_a[at], total_b[at]], axis=0).astype(jnp.bfloat16)


def in_columns(kernel, name, arrays, out_rows, out_types, early=()):
    width = arrays[0].shape[1]
    lanes = min(2048, width)

    def spec(rows):
        return pl.BlockSpec((rows, lanes), lambda i: (0, i))

    return pl.pallas_call(
        kernel,
        grid=(width // lanes,),
        in_specs=[spec(x.shape[0]) for x in arrays]
        + [pl.BlockSpec(x.shape, lambda i: (0, 0)) for x in early],
        out_specs=[spec(rows) for rows in out_rows],
        out_shape=[
            jax.ShapeDtypeStruct((rows, width), dtype) for rows, dtype in zip(out_rows, out_types)
        ],
        compiler_params=pltpu.CompilerParams(vmem_limit_bytes=VMEM),
        cost_estimate=SHORT,
        name=name,
    )(*arrays, *early)


def reduce_over_time(pieces, bits_a, bits_b, nlat, early):
    keep_a, send_a, keep_b, send_b = pieces
    for i, (bit_a, bit_b) in enumerate(zip(bits_a, bits_b)):
        got_a, got_b = swap_with(send_a, "tm", 1 << bit_a), swap_with(send_b, "tm", 1 << bit_b)
        arrays = [keep_a, got_a, keep_b, got_b]
        rows = keep_a.shape[0]
        if i < len(bits_a) - 1:
            keep_a, send_a, keep_b, send_b = in_columns(
                halve_kernel, "sum_step", arrays, [rows // 2] * 4, [jnp.float32, jnp.bfloat16] * 2,
                early if i == 0 else (),
            )
    owned = rows // nlat
    if owned % GROUP == 0:
        band = in_columns(
            finish_kernel, "sum_end", arrays, [2 * owned] * nlat, [jnp.bfloat16] * nlat
        )
    else:
        total_a, total_b = both_sums(*arrays)
        band = [
            jnp.concatenate([x[n * owned : (n + 1) * owned] for x in (total_a, total_b)]).astype(
                jnp.bfloat16
            )
            for n in range(nlat)
        ]
    return band, send_a


def after(x, *others):
    return lax.optimization_barrier((x,) + others)[0]


def from_here(orders, bits, my_tm, my_lat):
    levels, lat_levels = len(bits), orders.shape[1].bit_length() - 1
    x = orders.reshape((2,) * (levels + lat_levels) + orders.shape[2:])
    for axis in range(levels + lat_levels):
        here = my_tm >> (levels - 1 - axis) if axis < levels else my_lat >> (
            levels + lat_levels - 1 - axis
        )
        x = jnp.where(here & 1 == 1, jnp.flip(x, axis), x)
    order = [levels - 1 - bit for bit in bits] + list(range(levels, x.ndim))
    return x.transpose(order).reshape(-1)


def exchange(band, owned):
    out = []
    for offset, piece in enumerate(band):
        if offset:
            piece = swap_with(piece, "lat", offset)
        if owned < GROUP:
            width = piece.shape[1]
            piece = jnp.pad(
                piece.reshape(2, owned, width), ((0, 0), (0, GROUP - owned), (0, 0))
            ).reshape(2 * GROUP, width)
        out.append(piece)
    return out


def shards(frames, owner_map):
    frame_count, row_count, nlon = frames.shape
    order_count = owner_map.shape[0]
    nlat, ntm = lax.axis_size("lat"), lax.axis_size("tm")
    my_tm, my_lat = lax.axis_index("tm"), lax.axis_index("lat")
    south = my_lat >= nlat // 2
    levels = ntm.bit_length() - 1
    bits_a = list(range(levels))
    bits_b = bits_a[-1:] + bits_a[:-1]

    pairs = owner_map.reshape(nlat, ntm, -1, 2)
    owned = pairs.shape[2]
    small, large = jnp.min(pairs, axis=3), jnp.max(pairs, axis=3)
    wanted = jnp.concatenate(
        [
            from_here(x.transpose(1, 0, 2), b, my_tm, my_lat)
            for x, b in ((small, bits_a), (large, bits_b))
        ]
    )
    wanted = table_column(wanted, order_count)
    place = (wanted[:, None] == jnp.arange(order_count, dtype=jnp.int32)[None, :]).astype(
        jnp.bfloat16
    )
    tables = [jnp.asarray(t) for t in longitude_tables(nlon, order_count)]
    time_mats = jnp.asarray(time_matrices(frame_count, ntm))
    where = jnp.stack([south.astype(jnp.int32), my_tm.astype(jnp.int32)])

    mine = lax.dynamic_slice(pairs, (my_lat, my_tm, 0, 0), (1, 1, owned, 2))[0, 0]
    mine = jnp.stack([jnp.min(mine, axis=1), jnp.max(mine, axis=1)])
    mine = jnp.pad(mine, ((0, 0), (0, GROUP - owned)), mode="edge")
    parity = jnp.broadcast_to(mine[:, :, None], (2, GROUP, 128))
    here = jnp.stack([my_lat.astype(jnp.int32), my_tm.astype(jnp.int32)])

    quarter = row_count // ROWS // 4
    parts = [(sum(QUARTERS[:i]) * quarter, n * quarter) for i, n in enumerate(QUARTERS)]
    pieces = []
    for part in parts:
        if pieces:
            where = after(where, pieces[-1][0])
        pieces.append(transform_chunk(part, where, frames, tables, time_mats, place))
    bands, early, waits = [], [], []
    for i, piece in enumerate(pieces):
        if i == len(pieces) - 1:
            made = [
                polynomials(after(mine[g], *waits), g, order_count, nlat, row_count, parts)
                for g in range(2)
            ]
            early = [token for _, token in made]
        band, sent = reduce_over_time(piece, bits_a, bits_b, nlat, early)
        waits = [sent, pieces[-1][0]]
        bands.append(exchange(band, owned))
    lanes_at, acc = [0, 0], [None, None]
    spectra = []
    for i, (band, (_, blocks)) in enumerate(zip(bands, parts)):
        last = i == len(parts) - 1
        if i:
            band = [after(band[0], *acc)] + band[1:]
        for g in (1, 0):
            lanes = (nlat // 2 - g * nlat // 4) * blocks * ROWS
            acc[g] = contract_chunk(
                g, last, here, band, parity[g], made[g][0], lanes_at[g], lanes, acc[g],
                g * order_count // 2, ntm,
            )
            lanes_at[g] += lanes
    spectra = [[x[0]] + [swap_with(x[d], "tm", d) for d in range(1, ntm)] for x in acc]
    return arrange(here, owner_map, *spectra, owned)


def solution(mesh):
    return jax.shard_map(
        shards,
        mesh=mesh,
        in_specs=(P("tm", "lat", None), P()),
        out_specs=P(None, "lat", None, "tm"),
        check_vma=False,
    )
```

```python
from functools import partial
import math

import jax
import jax.numpy as jnp
import numpy as np
from jax import lax
from jax.experimental import pallas as pl
from jax.experimental.pallas import tpu as pltpu
from jax.sharding import PartitionSpec as P

L = 1024
F = 8
EF = 2 * F
ROWS = 16
WIDE = ROWS * EF
QUARTERS = (2, 2)
GROUP = 8
SPAN = 128
SPAN_OUT = 256
VMEM = 24 * 1024 * 1024
VMEM_LEGENDRE = 8 * 1024 * 1024
VMEM_SUM = 24 * 1024 * 1024


def longitude_tables(nlon, order_count):
    factor = np.float32(math.sqrt(2.0 / nlon))
    tables = []
    for first, stride, length in ((0, 4, nlon // 4), (2, 4, nlon // 4), (1, 2, nlon // 2)):
        points = np.arange(length, dtype=np.int64)[:, None]
        orders = np.arange(first, order_count, stride, dtype=np.int64)[None, :]
        angles = (orders * points % nlon).astype(np.float32) * np.float32(2.0 * math.pi / nlon)
        parts = [np.cos(angles) * factor, -np.sin(angles) * factor]
        tables.append(np.concatenate(parts, axis=1).astype(jnp.bfloat16))
    return tables


def table_column(orders, order_count):
    quarter = orders // 4 + orders % 4 // 2 * (order_count // 4)
    return jnp.where(orders % 2 == 1, order_count // 2 + orders // 2, quarter)


def time_matrices(frame_count, time_count):
    total = frame_count * time_count
    frames_at = np.arange(total, dtype=np.int64)
    frequency = total // 8 + np.arange(F, dtype=np.int64)
    phases = frequency[:, None] * frames_at[None, :] % total
    angles = phases.astype(np.float32) * np.float32(2.0 * math.pi / total)
    factor = np.float32(1.0 / math.sqrt(total))
    cos_part, sin_part = np.cos(angles) * factor, np.sin(angles) * factor
    weights = np.stack(
        [np.concatenate([cos_part, -sin_part]), np.concatenate([sin_part, cos_part])]
    )
    weights = weights.reshape(2, EF, time_count, frame_count).transpose(2, 0, 1, 3)
    same = np.stack([np.eye(ROWS), np.eye(ROWS)[::-1]]).astype(np.float32)
    full = weights[:, None, :, None, :, :, None] * same[None, :, None, :, None, None, :]
    return full.reshape(time_count, 2, 2, WIDE, frame_count * ROWS).astype(jnp.bfloat16)


SHORT = pl.CostEstimate(flops=10**6, bytes_accessed=10**5, transcendentals=0)


def product(a, b):
    return jnp.dot(a, b, preferred_element_type=jnp.float32)


def transform_kernel(where_ref, frames_ref, fours_ref, twos_ref, odd_ref, time_ref, place_ref, *refs):
    frame_count, rows, nlon = frames_ref.shape
    outs, (sum_s, diff_s, odd_s) = refs[:4], refs[4:]
    half, quarter = nlon // 2, nlon // 4
    count = rows // ROWS
    tall = frame_count * ROWS
    for i in range(count):
        at = slice(i * tall, (i + 1) * tall)
        first = jnp.where(where_ref[0] == 1, count - 1 - i, i) * ROWS
        image = frames_ref[:, pl.ds(pl.multiple_of(first, ROWS), ROWS), :].reshape(tall, nlon)
        near, far = image[:, :half], image[:, half:]
        even = near + far
        odd_s[at] = near - far
        sum_s[at] = even[:, :quarter] + even[:, quarter:]
        diff_s[at] = even[:, :quarter] - even[:, quarter:]
    coefs = [
        product(folded[...], table_ref[...]).astype(jnp.bfloat16)
        for folded, table_ref in ((sum_s, fours_ref), (diff_s, twos_ref), (odd_s, odd_ref))
    ]
    for i in range(count):
        bands = []
        for coef in coefs:
            coef = coef[i * tall : (i + 1) * tall]
            middle = coef.shape[1] // 2
            bands.append(
                product(time_ref[0, 0, 0], coef[:, :middle])
                + product(time_ref[0, 0, 1], coef[:, middle:])
            )
        band = jnp.concatenate(bands, axis=1).astype(jnp.bfloat16)
        placed = lax.dot_general(
            place_ref[...], band, (((1,), (1,)), ((), ())), preferred_element_type=jnp.float32
        ).astype(jnp.bfloat16)
        size = outs[0].shape[0]
        for n, out in enumerate(outs):
            out[:, i * WIDE : (i + 1) * WIDE] = placed[n * size : (n + 1) * size]


def transform_chunk(part, where, frames, tables, time_mats, place):
    frame_count, row_count, nlon = frames.shape
    first, blocks = part
    together = 2 if first % 2 == 0 and blocks % 2 == 0 else 1
    rows = together * ROWS
    steps, first, all_steps = blocks // together, first // together, row_count // rows
    order_count = place.shape[0]
    size = order_count // 4

    def frame_block(b, where_ref):
        at = first + b
        return (0, jnp.where(where_ref[0] == 1, all_steps - 1 - at, at), 0)

    def time_block(b, where_ref):
        return (where_ref[1], where_ref[0], 0, 0, 0)

    out = pltpu.HBM((size, blocks * WIDE), jnp.bfloat16)
    tall = frame_count * rows
    in_vmem = pl.BlockSpec(memory_space=pltpu.VMEM)
    return pl.pallas_call(
        transform_kernel,
        grid_spec=pltpu.PrefetchScalarGridSpec(
            num_scalar_prefetch=1,
            grid=(steps,),
            in_specs=[
                pl.BlockSpec((frame_count, rows, nlon), frame_block),
                *([in_vmem] * len(tables)),
                pl.BlockSpec((1, 1) + time_mats.shape[2:], time_block),
                in_vmem,
            ],
            out_specs=[pl.BlockSpec((size, rows * EF), lambda b, w: (0, b))] * 4,
            scratch_shapes=[
                pltpu.VMEM((tall, nlon // 4), jnp.bfloat16),
                pltpu.VMEM((tall, nlon // 4), jnp.bfloat16),
                pltpu.VMEM((tall, nlon // 2), jnp.bfloat16),
            ],
        ),
        out_shape=[out] * 4,
        compiler_params=pltpu.CompilerParams(vmem_limit_bytes=VMEM),
        cost_estimate=SHORT,
        name="longitude_time",
    )(where, frames, *tables, pltpu.with_memory_space_constraint(time_mats, pltpu.HBM), place)


def degree_factors(orders, level):
    level_sq = level * level
    order_sq = orders * orders
    lower = level - 1.0
    rising = jnp.sqrt(
        jnp.maximum(4.0 * level_sq - 1.0, 0.0) / jnp.maximum(level_sq - order_sq, 1.0)
    )
    falling = jnp.sqrt(
        jnp.maximum(lower * lower - order_sq, 0.0) / jnp.maximum(4.0 * lower * lower - 1.0, 1.0)
    )
    return rising, rising * falling


def polynomial_kernel(half, begin, orders_ref, growth_ref, rows_ref, out, token, state):
    step = pl.program_id(0)
    base = begin + step * SPAN
    order_count = growth_ref.shape[1]

    def spread(row):
        return jnp.broadcast_to(row, (GROUP, row.shape[1]))

    @pl.when(step == 0)
    def _():
        steps_k = lax.broadcasted_iota(jnp.int32, (GROUP, order_count), 1).astype(jnp.float32) + 1.0
        order = orders_ref[:, :1]
        growth = jnp.sum(
            jnp.where(steps_k <= order, spread(growth_ref[...]), 0.0), axis=1, keepdims=True
        )
        lognorm = 0.5 * math.log(0.5) + 0.5 * growth + order * spread(rows_ref[1:2])
        start = jnp.where(lognorm >= -60.0, jnp.exp(jnp.maximum(lognorm, -60.0)), 0.0)
        token[...] = jnp.zeros_like(token)
        state[0] = jnp.zeros_like(start)
        state[1] = jnp.zeros_like(start)
        state[2] = start * spread(rows_ref[2:3])

    x = spread(rows_ref[0:1])

    def run(begins):
        level = (lax.broadcasted_iota(jnp.int32, (GROUP, SPAN), 1) + base).astype(jnp.float32)
        rise, fall = degree_factors(orders_ref[...], level)
        older, last = state[0], state[1]
        first = pl.multiple_of(step * SPAN * GROUP, SPAN * GROUP)
        for at in range(0, SPAN, 2):
            made = []
            for i in (at, at + 1):
                new = (rise[:, i : i + 1] * x) * last - fall[:, i : i + 1] * older
                if begins:
                    here = jnp.where(orders_ref[...] == (base + i).astype(jnp.float32), 1.0, 0.0)
                    new = new + here[:, :1] * state[2]
                older, last = last, new
                made.append(new)
            both = jnp.concatenate(made, axis=0).astype(jnp.bfloat16)
            out[pl.ds(first + GROUP * at, 2 * GROUP), :] = both
        state[0], state[1] = older, last

    @pl.when(step < half)
    def _():
        run(True)

    @pl.when(step >= half)
    def _():
        run(False)


def polynomials(orders, which, order_count, nlat, rows_each, parts):
    nlat_count = nlat * rows_each
    half = order_count // 2 // SPAN
    rows = np.arange(nlat_count // 2).reshape(nlat // 2, rows_each)[which * nlat // 4 :]
    rows = np.concatenate(
        [rows[:, at * ROWS : (at + count) * ROWS].reshape(-1) for at, count in parts]
    )
    begin = which * order_count // 2
    colatitude = (rows.astype(np.float32) + np.float32(0.5)) * np.float32(math.pi / nlat_count)
    sine = np.sin(colatitude)
    weight = sine * np.float32(math.pi / nlat_count) * np.float32(math.sqrt(nlat_count))
    row_values = np.stack([np.cos(colatitude), np.log(sine), weight])
    growth = np.log1p(np.float32(0.5) / np.arange(1, order_count + 1, dtype=np.float32))[None, :]
    orders = jnp.broadcast_to(orders.astype(jnp.float32)[:, None], (GROUP, 128))

    def fixed(shape):
        return pl.BlockSpec(shape, lambda s: (0,) * len(shape))

    return pl.pallas_call(
        partial(polynomial_kernel, half, begin),
        grid=((L - begin) // SPAN,),
        in_specs=[fixed(orders.shape), fixed(growth.shape), fixed(row_values.shape)],
        out_specs=[pl.BlockSpec(memory_space=pltpu.VMEM), fixed((GROUP, 128))],
        out_shape=[
            jax.ShapeDtypeStruct(((L - begin) * GROUP, rows.size), jnp.bfloat16),
            jax.ShapeDtypeStruct((GROUP, 128), jnp.float32),
        ],
        scratch_shapes=[pltpu.VMEM((3, GROUP, rows.size), jnp.float32)],
        compiler_params=pltpu.CompilerParams(vmem_limit_bytes=VMEM_LEGENDRE),
        cost_estimate=SHORT,
        name="legendre",
    )(orders, jnp.asarray(growth), jnp.asarray(row_values))


def swap_groups(x):
    sub = lax.broadcasted_iota(jnp.int32, x.shape, 1)
    lane = lax.broadcasted_iota(jnp.int32, x.shape, 2) // EF
    for bit in (1, 2, 4):
        down = pltpu.roll(pltpu.roll(x, 8 - bit, 1), EF * bit, 2)
        up = pltpu.roll(pltpu.roll(x, bit, 1), 128 - EF * bit, 2)
        sub_on, lane_on = (sub & bit) != 0, (lane & bit) != 0
        x = jnp.where(sub_on == lane_on, x, jnp.where(sub_on, up, down))
    return x


def contract_kernel(halves, last, has_acc, nlat, span, lanes_at, here_ref, *refs):
    z_refs, parity_ref, p_refs = refs[:nlat], refs[nlat], refs[nlat + 1 : nlat + 3]
    refs = refs[nlat + 3 :]
    acc_refs, refs = (refs[:2], refs[2:]) if has_acc else ((), refs)
    out_refs, (z_all, *w_refs) = refs[:-3], refs[-3:]
    lanes = z_all.shape[2]
    for n, z_ref in enumerate(z_refs):
        z_all[n] = z_ref[...]

    def source(s, g):
        return z_all[s ^ here_ref[0]].astype(jnp.float32)[g * GROUP : (g + 1) * GROUP]

    for g, w_ref in enumerate(w_refs):
        for part, sign in ((0, 1.0), (1, -1.0)):
            pieces = []
            for s in range(g * nlat // 4, nlat // 2):
                both = source(s, g) + sign * source(nlat - 1 - s, g)
                pieces += [both[:, i : i + 128] for i in range(0, lanes, 128)]
            block = swap_groups(jnp.stack(pieces, axis=0))
            w_ref[:, part * 128 : (part + 1) * 128] = block.reshape(
                len(pieces) * GROUP, 128
            ).astype(jnp.bfloat16)

    sub = lax.broadcasted_iota(jnp.int32, (GROUP, 128), 0)
    lane = lax.broadcasted_iota(jnp.int32, (GROUP, 128), 1) // EF

    def own_columns(g, first):
        odd = [((parity_ref[g] + u) & 1) == 1 for u in range(2)]
        many = 16 if span % 128 == 0 else 4
        tile = many * GROUP * GROUP
        out = []
        for i in range(0, span * GROUP, tile):
            rows = p_refs[g][pl.ds(first + i, tile), lanes_at[g] : lanes_at[g] + w_refs[g].shape[0]]
            full = product(rows, w_refs[g][...]).reshape(many, GROUP, GROUP, 256)
            kept = None
            for n in range(GROUP):
                one = jnp.where(odd[n % 2], full[:, n, :, 128:], full[:, n, :, :128])
                if n == 0:
                    kept = one
                else:
                    kept = jnp.where(((sub - lane) & 7) == n, pltpu.roll(one, n, 1), kept)
            for bit in (1, 2, 4):
                kept = jnp.where((lane & bit) != 0, pltpu.roll(kept, GROUP - bit, 1), kept)
            out.append(kept.reshape(many * GROUP, 128))
        return jnp.concatenate(out, axis=0)

    def put(step, g, value):
        per = out_refs[0].shape[1] // span
        for offset, out_ref in enumerate(out_refs):
            for i in range(per):

                @pl.when(((step // per) ^ here_ref[1] == offset) & (step % per == i))
                def _():
                    out_ref[g * 128 : (g + 1) * 128, i * span : (i + 1) * span] = value

    for g, half in enumerate(halves):
        if last and half:

            @pl.loop(0, half)
            def _(step):
                put(step, g, jnp.zeros((128, span), jnp.bfloat16))

        @pl.loop(half, L // span)
        def _(step):
            value = own_columns(g, pl.multiple_of((step - half) * span * GROUP, 256))
            at = pl.ds(pl.multiple_of((step - half) * span, span), span)
            if has_acc:
                value = value + acc_refs[g][at, :]
            if last:
                put(step, g, value.T.astype(jnp.bfloat16))
            else:
                out_refs[g][at, :] = value


def contract_chunk(last, here, z, parity, p, lanes_at, lanes, acc, begins, ntm):
    each = L // ntm
    span = min(SPAN_OUT, each)
    if last:
        out_shape = [jax.ShapeDtypeStruct((256, each), jnp.bfloat16)] * ntm
    else:
        out_shape = [jax.ShapeDtypeStruct((L - begin, 128), jnp.float32) for begin in begins]

    def whole(x):
        return pl.BlockSpec(x.shape, lambda s, _: (0,) * len(x.shape))

    halves = [begin // span for begin in begins]
    return pl.pallas_call(
        partial(contract_kernel, halves, last, bool(acc), len(z), span, lanes_at),
        grid_spec=pltpu.PrefetchScalarGridSpec(
            num_scalar_prefetch=1,
            grid=(1,),
            in_specs=[whole(x) for x in (*z, parity)]
            + [pl.BlockSpec(memory_space=pltpu.VMEM)] * 2
            + [whole(x) for x in acc],
            out_specs=[whole(x) for x in out_shape],
            scratch_shapes=[
                pltpu.VMEM((len(z),) + z[0].shape, jnp.bfloat16),
                *(pltpu.VMEM((n, 256), jnp.bfloat16) for n in lanes),
            ],
        ),
        out_shape=out_shape,
        compiler_params=pltpu.CompilerParams(vmem_limit_bytes=VMEM_SUM),
        cost_estimate=SHORT,
        name="latitude_sum",
    )(here, *z, parity, *p, *acc)


def arrange_kernel(owned, here_ref, orders_ref, *refs):
    out_ref = refs[-1]
    count = len(refs) - 1
    for offset in range(count):
        source = offset ^ here_ref[1]
        sums = refs[offset][...].astype(jnp.float32)
        low, high = sums[:128], sums[128:]
        for i in range(owned):
            first = orders_ref[((here_ref[0] * count + source) * owned + i) * 2]
            in_order = first < orders_ref.shape[0] // 2
            for e in range(2):
                a, b = low[i * EF + e * F :][:F], high[i * EF + e * F :][:F]
                slot = (source * owned + i) * 2
                out_ref[e, slot] = jnp.where(in_order, a, b)
                out_ref[e, slot + 1] = jnp.where(in_order, b, a)


def arrange(here, owner_map, sums, owned):
    ntm, each = len(sums), sums[0].shape[1]
    return pl.pallas_call(
        partial(arrange_kernel, owned),
        grid_spec=pltpu.PrefetchScalarGridSpec(
            num_scalar_prefetch=2,
            grid=(1,),
            in_specs=[pl.BlockSpec((256, each), lambda s, h, f: (0, 0))] * ntm,
            out_specs=pl.BlockSpec((2, ntm * owned * 2, F, each), lambda s, h, f: (0, 0, 0, 0)),
        ),
        out_shape=jax.ShapeDtypeStruct((2, ntm * owned * 2, F, each), jnp.float32),
        name="slot_order",
    )(here, owner_map, *sums)


def swap_with(x, axis, offset):
    count = lax.axis_size(axis)
    return lax.ppermute(x, axis, [(i, i ^ offset) for i in range(count)])


def both_sums(keep_a, got_a, keep_b, got_b):
    return [
        k[...].astype(jnp.float32) + g[...].astype(jnp.float32)
        for k, g in ((keep_a, got_a), (keep_b, got_b))
    ]


def halve_kernel(keep_a, got_a, keep_b, got_b, *outs):
    outs = outs[-4:]
    for n, total in enumerate(both_sums(keep_a, got_a, keep_b, got_b)):
        middle = total.shape[0] // 2
        outs[2 * n][...] = total[:middle]
        outs[2 * n + 1][...] = total[middle:].astype(jnp.bfloat16)


def finish_kernel(keep_a, got_a, keep_b, got_b, *outs):
    total_a, total_b = both_sums(keep_a, got_a, keep_b, got_b)
    owned = total_a.shape[0] // len(outs)
    for n, out in enumerate(outs):
        at = slice(n * owned, (n + 1) * owned)
        out[...] = jnp.concatenate([total_a[at], total_b[at]], axis=0).astype(jnp.bfloat16)


def in_columns(kernel, name, arrays, out_rows, out_types, early=()):
    width = arrays[0].shape[1]
    lanes = width

    def spec(rows):
        return pl.BlockSpec((rows, lanes), lambda i: (0, i))

    return pl.pallas_call(
        kernel,
        grid=(width // lanes,),
        in_specs=[spec(x.shape[0]) for x in arrays]
        + [pl.BlockSpec(x.shape, lambda i: (0, 0)) for x in early],
        out_specs=[spec(rows) for rows in out_rows],
        out_shape=[
            jax.ShapeDtypeStruct((rows, width), dtype) for rows, dtype in zip(out_rows, out_types)
        ],
        compiler_params=pltpu.CompilerParams(vmem_limit_bytes=VMEM),
        cost_estimate=SHORT,
        name=name,
    )(*arrays, *early)


def reduce_over_time(pieces, bits_a, bits_b, nlat, early):
    keep_a, send_a, keep_b, send_b = pieces
    for i, (bit_a, bit_b) in enumerate(zip(bits_a, bits_b)):
        got_a, got_b = swap_with(send_a, "tm", 1 << bit_a), swap_with(send_b, "tm", 1 << bit_b)
        arrays = [keep_a, got_a, keep_b, got_b]
        rows = keep_a.shape[0]
        if i < len(bits_a) - 1:
            keep_a, send_a, keep_b, send_b = in_columns(
                halve_kernel, "sum_step", arrays, [rows // 2] * 4, [jnp.float32, jnp.bfloat16] * 2,
                early if i == 0 else (),
            )
    owned = rows // nlat
    if owned % GROUP == 0:
        band = in_columns(
            finish_kernel, "sum_end", arrays, [2 * owned] * nlat, [jnp.bfloat16] * nlat
        )
    else:
        total_a, total_b = both_sums(*arrays)
        band = [
            jnp.concatenate([x[n * owned : (n + 1) * owned] for x in (total_a, total_b)]).astype(
                jnp.bfloat16
            )
            for n in range(nlat)
        ]
    return band, send_a


def after(x, *others):
    return lax.optimization_barrier((x,) + others)[0]


def from_here(orders, bits, my_tm, my_lat):
    levels, lat_levels = len(bits), orders.shape[1].bit_length() - 1
    x = orders.reshape((2,) * (levels + lat_levels) + orders.shape[2:])
    for axis in range(levels + lat_levels):
        here = my_tm >> (levels - 1 - axis) if axis < levels else my_lat >> (
            levels + lat_levels - 1 - axis
        )
        x = jnp.where(here & 1 == 1, jnp.flip(x, axis), x)
    order = [levels - 1 - bit for bit in bits] + list(range(levels, x.ndim))
    return x.transpose(order).reshape(-1)


def exchange(band, owned, offsets):
    out = {}
    for offset in offsets:
        piece = band[offset]
        if offset:
            piece = swap_with(piece, "lat", offset)
        if owned < GROUP:
            width = piece.shape[1]
            piece = jnp.pad(
                piece.reshape(2, owned, width), ((0, 0), (0, GROUP - owned), (0, 0))
            ).reshape(2 * GROUP, width)
        out[offset] = piece
    return [out[offset] for offset in sorted(out)]


def shards(frames, owner_map):
    frame_count, row_count, nlon = frames.shape
    order_count = owner_map.shape[0]
    nlat, ntm = lax.axis_size("lat"), lax.axis_size("tm")
    my_tm, my_lat = lax.axis_index("tm"), lax.axis_index("lat")
    south = my_lat >= nlat // 2
    levels = ntm.bit_length() - 1
    bits_a = list(range(levels))
    bits_b = bits_a[-1:] + bits_a[:-1]

    pairs = owner_map.reshape(nlat, ntm, -1, 2)
    owned = pairs.shape[2]
    small, large = jnp.min(pairs, axis=3), jnp.max(pairs, axis=3)
    wanted = jnp.concatenate(
        [
            from_here(x.transpose(1, 0, 2), b, my_tm, my_lat)
            for x, b in ((small, bits_a), (large, bits_b))
        ]
    )
    wanted = table_column(wanted, order_count)
    place = (wanted[:, None] == jnp.arange(order_count, dtype=jnp.int32)[None, :]).astype(
        jnp.bfloat16
    )
    tables = [jnp.asarray(t) for t in longitude_tables(nlon, order_count)]
    time_mats = jnp.asarray(time_matrices(frame_count, ntm))
    where = jnp.stack([south.astype(jnp.int32), my_tm.astype(jnp.int32)])

    mine = lax.dynamic_slice(pairs, (my_lat, my_tm, 0, 0), (1, 1, owned, 2))[0, 0]
    mine = jnp.stack([jnp.min(mine, axis=1), jnp.max(mine, axis=1)])
    mine = jnp.pad(mine, ((0, 0), (0, GROUP - owned)), mode="edge")
    parity = jnp.broadcast_to(mine[:, :, None], (2, GROUP, 128))
    here = jnp.stack([my_lat.astype(jnp.int32), my_tm.astype(jnp.int32)])

    quarter = row_count // ROWS // 4
    parts = [(sum(QUARTERS[:i]) * quarter, n * quarter) for i, n in enumerate(QUARTERS)]
    pieces = []
    for part in parts:
        if pieces:
            where = after(where, pieces[-1][0])
        pieces.append(transform_chunk(part, where, frames, tables, time_mats, place))
    bands, early, waits = [], [], []
    for i, piece in enumerate(pieces):
        if i == len(pieces) - 1:
            made = [
                polynomials(after(mine[g], *waits), g, order_count, nlat, row_count, parts)
                for g in range(2)
            ]
            early = [token for _, token in made]
        band, sent = reduce_over_time(piece, bits_a, bits_b, nlat, early)
        waits = [sent, pieces[-1][0]]
        bands.append(band)
    lanes_at, acc = (0, 0), ()
    for i, (band, (_, blocks)) in enumerate(zip(bands, parts)):
        band = exchange(band, owned, range(nlat - 1, -1, -1))
        if acc:
            band = [after(band[0], *acc), *band[1:]]
        lanes = [(nlat // 2 - g * nlat // 4) * blocks * ROWS for g in range(2)]
        acc = contract_chunk(
            i == len(parts) - 1, here, band, parity, [m[0] for m in made], lanes_at, lanes,
            acc, (0, order_count // 2), ntm,
        )
        lanes_at = tuple(x + y for x, y in zip(lanes_at, lanes))
    sums = [acc[0]] + [swap_with(acc[d], "tm", d) for d in range(1, ntm)]
    return arrange(here, owner_map, sums, owned)


def solution(mesh):
    return jax.shard_map(
        shards,
        mesh=mesh,
        in_specs=(P("tm", "lat", None), P()),
        out_specs=P(None, "lat", None, "tm"),
        check_vma=False,
    )
```

```python
from functools import partial
import math

import jax
import jax.numpy as jnp
import numpy as np
from jax import lax
from jax.experimental import pallas as pl
from jax.experimental.pallas import tpu as pltpu
from jax.sharding import PartitionSpec as P

L = 1024
F = 8
EF = 2 * F
ROWS = 16
WIDE = ROWS * EF
QUARTERS = (2, 2)
GROUP = 8
SPAN = 128
SPAN_OUT = 256
VMEM = 24 * 1024 * 1024
VMEM_LEGENDRE = 8 * 1024 * 1024
VMEM_SUM = 24 * 1024 * 1024


def longitude_tables(nlon, order_count):
    factor = np.float32(math.sqrt(2.0 / nlon))
    tables = []
    for first, stride, length in ((0, 4, nlon // 4), (2, 4, nlon // 4), (1, 2, nlon // 2)):
        points = np.arange(length, dtype=np.int64)[:, None]
        orders = np.arange(first, order_count, stride, dtype=np.int64)[None, :]
        angles = (orders * points % nlon).astype(np.float32) * np.float32(2.0 * math.pi / nlon)
        parts = [np.cos(angles) * factor, -np.sin(angles) * factor]
        tables.append(np.concatenate(parts, axis=1).astype(jnp.bfloat16))
    return tables


def table_column(orders, order_count):
    quarter = orders // 4 + orders % 4 // 2 * (order_count // 4)
    return jnp.where(orders % 2 == 1, order_count // 2 + orders // 2, quarter)


def time_matrices(frame_count, time_count):
    total = frame_count * time_count
    frames_at = np.arange(total, dtype=np.int64)
    frequency = total // 8 + np.arange(F, dtype=np.int64)
    phases = frequency[:, None] * frames_at[None, :] % total
    angles = phases.astype(np.float32) * np.float32(2.0 * math.pi / total)
    factor = np.float32(1.0 / math.sqrt(total))
    cos_part, sin_part = np.cos(angles) * factor, np.sin(angles) * factor
    weights = np.stack(
        [np.concatenate([cos_part, -sin_part]), np.concatenate([sin_part, cos_part])]
    )
    weights = weights.reshape(2, EF, time_count, frame_count).transpose(2, 0, 1, 3)
    same = np.stack([np.eye(ROWS), np.eye(ROWS)[::-1]]).astype(np.float32)
    full = weights[:, None, :, None, :, :, None] * same[None, :, None, :, None, None, :]
    return full.reshape(time_count, 2, 2, WIDE, frame_count * ROWS).astype(jnp.bfloat16)


SHORT = pl.CostEstimate(flops=10**6, bytes_accessed=10**5, transcendentals=0)


def product(a, b):
    return jnp.dot(a, b, preferred_element_type=jnp.float32)


def transform_kernel(where_ref, frames_ref, fours_ref, twos_ref, odd_ref, time_ref, place_ref, *refs):
    frame_count, rows, nlon = frames_ref.shape
    outs, (sum_s, diff_s, odd_s) = refs[:4], refs[4:]
    half, quarter = nlon // 2, nlon // 4
    count = rows // ROWS
    tall = frame_count * ROWS
    for i in range(count):
        at = slice(i * tall, (i + 1) * tall)
        first = jnp.where(where_ref[0] == 1, count - 1 - i, i) * ROWS
        image = frames_ref[:, pl.ds(pl.multiple_of(first, ROWS), ROWS), :].reshape(tall, nlon)
        near, far = image[:, :half], image[:, half:]
        even = near + far
        odd_s[at] = near - far
        sum_s[at] = even[:, :quarter] + even[:, quarter:]
        diff_s[at] = even[:, :quarter] - even[:, quarter:]
    coefs = [
        product(folded[...], table_ref[...]).astype(jnp.bfloat16)
        for folded, table_ref in ((sum_s, fours_ref), (diff_s, twos_ref), (odd_s, odd_ref))
    ]
    for i in range(count):
        at = slice(i * tall, (i + 1) * tall)
        cosines = [coef[at, : coef.shape[1] // 2] for coef in coefs]
        sines = [coef[at, coef.shape[1] // 2 :] for coef in coefs]
        stacked = jnp.concatenate(
            [jnp.concatenate(cosines, axis=1), jnp.concatenate(sines, axis=1)], axis=0
        )
        both = jnp.concatenate([time_ref[0, 0, 0], time_ref[0, 0, 1]], axis=1)
        band = product(both, stacked).astype(jnp.bfloat16)
        placed = lax.dot_general(
            place_ref[...], band, (((1,), (1,)), ((), ())), preferred_element_type=jnp.float32
        ).astype(jnp.bfloat16)
        size = outs[0].shape[0]
        for n, out in enumerate(outs):
            out[:, i * WIDE : (i + 1) * WIDE] = placed[n * size : (n + 1) * size]


def transform_chunk(part, where, frames, tables, time_mats, place):
    frame_count, row_count, nlon = frames.shape
    first, blocks = part
    together = 2 if first % 2 == 0 and blocks % 2 == 0 else 1
    rows = together * ROWS
    steps, first, all_steps = blocks // together, first // together, row_count // rows
    order_count = place.shape[0]
    size = order_count // 4

    def frame_block(b, where_ref):
        at = first + b
        return (0, jnp.where(where_ref[0] == 1, all_steps - 1 - at, at), 0)

    def time_block(b, where_ref):
        return (where_ref[1], where_ref[0], 0, 0, 0)

    out = pltpu.HBM((size, blocks * WIDE), jnp.bfloat16)
    tall = frame_count * rows
    in_vmem = pl.BlockSpec(memory_space=pltpu.VMEM)
    return pl.pallas_call(
        transform_kernel,
        grid_spec=pltpu.PrefetchScalarGridSpec(
            num_scalar_prefetch=1,
            grid=(steps,),
            in_specs=[
                pl.BlockSpec((frame_count, rows, nlon), frame_block),
                *([in_vmem] * len(tables)),
                pl.BlockSpec((1, 1) + time_mats.shape[2:], time_block),
                in_vmem,
            ],
            out_specs=[pl.BlockSpec((size, rows * EF), lambda b, w: (0, b))] * 4,
            scratch_shapes=[
                pltpu.VMEM((tall, nlon // 4), jnp.bfloat16),
                pltpu.VMEM((tall, nlon // 4), jnp.bfloat16),
                pltpu.VMEM((tall, nlon // 2), jnp.bfloat16),
            ],
        ),
        out_shape=[out] * 4,
        compiler_params=pltpu.CompilerParams(vmem_limit_bytes=VMEM),
        cost_estimate=SHORT,
        name="longitude_time",
    )(where, frames, *tables, pltpu.with_memory_space_constraint(time_mats, pltpu.HBM), place)


def degree_factors(orders, level):
    level_sq = level * level
    order_sq = orders * orders
    lower = level - 1.0
    rising = jnp.sqrt(
        jnp.maximum(4.0 * level_sq - 1.0, 0.0) / jnp.maximum(level_sq - order_sq, 1.0)
    )
    falling = jnp.sqrt(
        jnp.maximum(lower * lower - order_sq, 0.0) / jnp.maximum(4.0 * lower * lower - 1.0, 1.0)
    )
    return rising, rising * falling


def polynomial_kernel(half, begin, orders_ref, growth_ref, rows_ref, out, token, state):
    step = pl.program_id(0)
    base = begin + step * SPAN
    order_count = growth_ref.shape[1]

    def spread(row):
        return jnp.broadcast_to(row, (GROUP, row.shape[1]))

    @pl.when(step == 0)
    def _():
        steps_k = lax.broadcasted_iota(jnp.int32, (GROUP, order_count), 1).astype(jnp.float32) + 1.0
        order = orders_ref[:, :1]
        growth = jnp.sum(
            jnp.where(steps_k <= order, spread(growth_ref[...]), 0.0), axis=1, keepdims=True
        )
        lognorm = 0.5 * math.log(0.5) + 0.5 * growth + order * spread(rows_ref[1:2])
        start = jnp.where(lognorm >= -60.0, jnp.exp(jnp.maximum(lognorm, -60.0)), 0.0)
        token[...] = jnp.zeros_like(token)
        state[0] = jnp.zeros_like(start)
        state[1] = jnp.zeros_like(start)
        state[2] = start * spread(rows_ref[2:3])

    x = spread(rows_ref[0:1])

    def run(begins):
        level = (lax.broadcasted_iota(jnp.int32, (GROUP, SPAN), 1) + base).astype(jnp.float32)
        rise, fall = degree_factors(orders_ref[...], level)
        older, last = state[0], state[1]
        first = pl.multiple_of(step * SPAN * GROUP, SPAN * GROUP)
        for at in range(0, SPAN, 2):
            made = []
            for i in (at, at + 1):
                new = (rise[:, i : i + 1] * x) * last - fall[:, i : i + 1] * older
                if begins:
                    here = jnp.where(orders_ref[...] == (base + i).astype(jnp.float32), 1.0, 0.0)
                    new = new + here[:, :1] * state[2]
                older, last = last, new
                made.append(new)
            both = jnp.concatenate(made, axis=0).astype(jnp.bfloat16)
            out[pl.ds(first + GROUP * at, 2 * GROUP), :] = both
        state[0], state[1] = older, last

    @pl.when(step < half)
    def _():
        run(True)

    @pl.when(step >= half)
    def _():
        run(False)


def polynomials(orders, which, order_count, nlat, rows_each, parts):
    nlat_count = nlat * rows_each
    half = order_count // 2 // SPAN
    rows = np.arange(nlat_count // 2).reshape(nlat // 2, rows_each)[which * nlat // 4 :]
    rows = np.concatenate(
        [rows[:, at * ROWS : (at + count) * ROWS].reshape(-1) for at, count in parts]
    )
    begin = which * order_count // 2
    colatitude = (rows.astype(np.float32) + np.float32(0.5)) * np.float32(math.pi / nlat_count)
    sine = np.sin(colatitude)
    weight = sine * np.float32(math.pi / nlat_count) * np.float32(math.sqrt(nlat_count))
    row_values = np.stack([np.cos(colatitude), np.log(sine), weight])
    growth = np.log1p(np.float32(0.5) / np.arange(1, order_count + 1, dtype=np.float32))[None, :]
    orders = jnp.broadcast_to(orders.astype(jnp.float32)[:, None], (GROUP, 128))

    def fixed(shape):
        return pl.BlockSpec(shape, lambda s: (0,) * len(shape))

    return pl.pallas_call(
        partial(polynomial_kernel, half, begin),
        grid=((L - begin) // SPAN,),
        in_specs=[fixed(orders.shape), fixed(growth.shape), fixed(row_values.shape)],
        out_specs=[pl.BlockSpec(memory_space=pltpu.VMEM), fixed((GROUP, 128))],
        out_shape=[
            jax.ShapeDtypeStruct(((L - begin) * GROUP, rows.size), jnp.bfloat16),
            jax.ShapeDtypeStruct((GROUP, 128), jnp.float32),
        ],
        scratch_shapes=[pltpu.VMEM((3, GROUP, rows.size), jnp.float32)],
        compiler_params=pltpu.CompilerParams(vmem_limit_bytes=VMEM_LEGENDRE),
        cost_estimate=SHORT,
        name="legendre",
    )(orders, jnp.asarray(growth), jnp.asarray(row_values))


def swap_groups(x):
    sub = lax.broadcasted_iota(jnp.int32, x.shape, 1)
    lane = lax.broadcasted_iota(jnp.int32, x.shape, 2) // EF
    for bit in (1, 2, 4):
        down = pltpu.roll(pltpu.roll(x, 8 - bit, 1), EF * bit, 2)
        up = pltpu.roll(pltpu.roll(x, bit, 1), 128 - EF * bit, 2)
        sub_on, lane_on = (sub & bit) != 0, (lane & bit) != 0
        x = jnp.where(sub_on == lane_on, x, jnp.where(sub_on, up, down))
    return x


def contract_kernel(halves, last, has_acc, nlat, span, lanes_at, here_ref, *refs):
    z_refs, parity_ref, p_refs = refs[:nlat], refs[nlat], refs[nlat + 1 : nlat + 3]
    refs = refs[nlat + 3 :]
    acc_refs, refs = (refs[:2], refs[2:]) if has_acc else ((), refs)
    out_refs, (z_all, *w_refs) = refs[:-3], refs[-3:]
    lanes = z_all.shape[2]
    for n, z_ref in enumerate(z_refs):
        z_all[n] = z_ref[...]

    def source(s, g):
        return z_all[s ^ here_ref[0]].astype(jnp.float32)[g * GROUP : (g + 1) * GROUP]

    for g, w_ref in enumerate(w_refs):
        for part, sign in ((0, 1.0), (1, -1.0)):
            pieces = []
            for s in range(g * nlat // 4, nlat // 2):
                both = source(s, g) + sign * source(nlat - 1 - s, g)
                pieces += [both[:, i : i + 128] for i in range(0, lanes, 128)]
            block = swap_groups(jnp.stack(pieces, axis=0))
            w_ref[:, part * 128 : (part + 1) * 128] = block.reshape(
                len(pieces) * GROUP, 128
            ).astype(jnp.bfloat16)

    sub = lax.broadcasted_iota(jnp.int32, (GROUP, 128), 0)
    lane = lax.broadcasted_iota(jnp.int32, (GROUP, 128), 1) // EF

    def own_columns(g, first):
        odd = [((parity_ref[g] + u) & 1) == 1 for u in range(2)]
        many = 16 if span % 128 == 0 else 4
        tile = many * GROUP * GROUP
        out = []
        for i in range(0, span * GROUP, tile):
            rows = p_refs[g][pl.ds(first + i, tile), lanes_at[g] : lanes_at[g] + w_refs[g].shape[0]]
            full = product(rows, w_refs[g][...]).reshape(many, GROUP, GROUP, 256)
            kept = None
            for n in range(GROUP):
                one = jnp.where(odd[n % 2], full[:, n, :, 128:], full[:, n, :, :128])
                if n == 0:
                    kept = one
                else:
                    kept = jnp.where(((sub - lane) & 7) == n, pltpu.roll(one, n, 1), kept)
            for bit in (1, 2, 4):
                kept = jnp.where((lane & bit) != 0, pltpu.roll(kept, GROUP - bit, 1), kept)
            out.append(kept.reshape(many * GROUP, 128))
        return jnp.concatenate(out, axis=0)

    def put(step, g, value):
        per = out_refs[0].shape[1] // span
        for offset, out_ref in enumerate(out_refs):
            for i in range(per):

                @pl.when(((step // per) ^ here_ref[1] == offset) & (step % per == i))
                def _():
                    out_ref[g * 128 : (g + 1) * 128, i * span : (i + 1) * span] = value

    for g, half in enumerate(halves):
        if last and half:

            @pl.loop(0, half)
            def _(step):
                put(step, g, jnp.zeros((128, span), jnp.bfloat16))

        @pl.loop(half, L // span)
        def _(step):
            value = own_columns(g, pl.multiple_of((step - half) * span * GROUP, 256))
            at = pl.ds(pl.multiple_of((step - half) * span, span), span)
            if has_acc:
                value = value + acc_refs[g][at, :]
            if last:
                put(step, g, value.T.astype(jnp.bfloat16))
            else:
                out_refs[g][at, :] = value


def contract_chunk(last, here, z, parity, p, lanes_at, lanes, acc, begins, ntm):
    each = L // ntm
    span = min(SPAN_OUT, each)
    if last:
        out_shape = [jax.ShapeDtypeStruct((256, each), jnp.bfloat16)] * ntm
    else:
        out_shape = [jax.ShapeDtypeStruct((L - begin, 128), jnp.float32) for begin in begins]

    def whole(x):
        return pl.BlockSpec(x.shape, lambda s, _: (0,) * len(x.shape))

    halves = [begin // span for begin in begins]
    return pl.pallas_call(
        partial(contract_kernel, halves, last, bool(acc), len(z), span, lanes_at),
        grid_spec=pltpu.PrefetchScalarGridSpec(
            num_scalar_prefetch=1,
            grid=(1,),
            in_specs=[whole(x) for x in (*z, parity)]
            + [pl.BlockSpec(memory_space=pltpu.VMEM)] * 2
            + [whole(x) for x in acc],
            out_specs=[whole(x) for x in out_shape],
            scratch_shapes=[
                pltpu.VMEM((len(z),) + z[0].shape, jnp.bfloat16),
                *(pltpu.VMEM((n, 256), jnp.bfloat16) for n in lanes),
            ],
        ),
        out_shape=out_shape,
        compiler_params=pltpu.CompilerParams(vmem_limit_bytes=VMEM_SUM),
        cost_estimate=SHORT,
        name="latitude_sum",
    )(here, *z, parity, *p, *acc)


def arrange_kernel(owned, here_ref, orders_ref, *refs):
    out_ref = refs[-1]
    count = len(refs) - 1
    for offset in range(count):
        source = offset ^ here_ref[1]
        sums = refs[offset][...].astype(jnp.float32)
        low, high = sums[:128], sums[128:]
        for i in range(owned):
            first = orders_ref[((here_ref[0] * count + source) * owned + i) * 2]
            in_order = first < orders_ref.shape[0] // 2
            for e in range(2):
                a, b = low[i * EF + e * F :][:F], high[i * EF + e * F :][:F]
                slot = (source * owned + i) * 2
                out_ref[e, slot] = jnp.where(in_order, a, b)
                out_ref[e, slot + 1] = jnp.where(in_order, b, a)


def arrange(here, owner_map, sums, owned):
    ntm, each = len(sums), sums[0].shape[1]
    return pl.pallas_call(
        partial(arrange_kernel, owned),
        grid_spec=pltpu.PrefetchScalarGridSpec(
            num_scalar_prefetch=2,
            grid=(1,),
            in_specs=[pl.BlockSpec((256, each), lambda s, h, f: (0, 0))] * ntm,
            out_specs=pl.BlockSpec((2, ntm * owned * 2, F, each), lambda s, h, f: (0, 0, 0, 0)),
        ),
        out_shape=jax.ShapeDtypeStruct((2, ntm * owned * 2, F, each), jnp.float32),
        name="slot_order",
    )(here, owner_map, *sums)


def swap_with(x, axis, offset):
    count = lax.axis_size(axis)
    return lax.ppermute(x, axis, [(i, i ^ offset) for i in range(count)])


def both_sums(keep_a, got_a, keep_b, got_b):
    return [
        k[...].astype(jnp.float32) + g[...].astype(jnp.float32)
        for k, g in ((keep_a, got_a), (keep_b, got_b))
    ]


def halve_kernel(keep_a, got_a, keep_b, got_b, *outs):
    outs = outs[-4:]
    for n, total in enumerate(both_sums(keep_a, got_a, keep_b, got_b)):
        middle = total.shape[0] // 2
        outs[2 * n][...] = total[:middle]
        outs[2 * n + 1][...] = total[middle:].astype(jnp.bfloat16)


def finish_kernel(keep_a, got_a, keep_b, got_b, *outs):
    total_a, total_b = both_sums(keep_a, got_a, keep_b, got_b)
    owned = total_a.shape[0] // len(outs)
    for n, out in enumerate(outs):
        at = slice(n * owned, (n + 1) * owned)
        out[...] = jnp.concatenate([total_a[at], total_b[at]], axis=0).astype(jnp.bfloat16)


def in_columns(kernel, name, arrays, out_rows, out_types, early=()):
    width = arrays[0].shape[1]
    lanes = width

    def spec(rows):
        return pl.BlockSpec((rows, lanes), lambda i: (0, i))

    return pl.pallas_call(
        kernel,
        grid=(width // lanes,),
        in_specs=[spec(x.shape[0]) for x in arrays]
        + [pl.BlockSpec(x.shape, lambda i: (0, 0)) for x in early],
        out_specs=[spec(rows) for rows in out_rows],
        out_shape=[
            jax.ShapeDtypeStruct((rows, width), dtype) for rows, dtype in zip(out_rows, out_types)
        ],
        compiler_params=pltpu.CompilerParams(vmem_limit_bytes=VMEM),
        cost_estimate=SHORT,
        name=name,
    )(*arrays, *early)


def reduce_over_time(pieces, bits_a, bits_b, nlat, early):
    keep_a, send_a, keep_b, send_b = pieces
    for i, (bit_a, bit_b) in enumerate(zip(bits_a, bits_b)):
        got_a, got_b = swap_with(send_a, "tm", 1 << bit_a), swap_with(send_b, "tm", 1 << bit_b)
        arrays = [keep_a, got_a, keep_b, got_b]
        rows = keep_a.shape[0]
        if i < len(bits_a) - 1:
            keep_a, send_a, keep_b, send_b = in_columns(
                halve_kernel, "sum_step", arrays, [rows // 2] * 4, [jnp.float32, jnp.bfloat16] * 2,
                early if i == 0 else (),
            )
    owned = rows // nlat
    if owned % GROUP == 0:
        band = in_columns(
            finish_kernel, "sum_end", arrays, [2 * owned] * nlat, [jnp.bfloat16] * nlat
        )
    else:
        total_a, total_b = both_sums(*arrays)
        band = [
            jnp.concatenate([x[n * owned : (n + 1) * owned] for x in (total_a, total_b)]).astype(
                jnp.bfloat16
            )
            for n in range(nlat)
        ]
    return band, send_a


def after(x, *others):
    return lax.optimization_barrier((x,) + others)[0]


def from_here(orders, bits, my_tm, my_lat):
    levels, lat_levels = len(bits), orders.shape[1].bit_length() - 1
    x = orders.reshape((2,) * (levels + lat_levels) + orders.shape[2:])
    for axis in range(levels + lat_levels):
        here = my_tm >> (levels - 1 - axis) if axis < levels else my_lat >> (
            levels + lat_levels - 1 - axis
        )
        x = jnp.where(here & 1 == 1, jnp.flip(x, axis), x)
    order = [levels - 1 - bit for bit in bits] + list(range(levels, x.ndim))
    return x.transpose(order).reshape(-1)


def exchange(band, owned, offsets):
    out = {}
    for offset in offsets:
        piece = band[offset]
        if offset:
            piece = swap_with(piece, "lat", offset)
        if owned < GROUP:
            width = piece.shape[1]
            piece = jnp.pad(
                piece.reshape(2, owned, width), ((0, 0), (0, GROUP - owned), (0, 0))
            ).reshape(2 * GROUP, width)
        out[offset] = piece
    return [out[offset] for offset in sorted(out)]


def shards(frames, owner_map):
    frame_count, row_count, nlon = frames.shape
    order_count = owner_map.shape[0]
    nlat, ntm = lax.axis_size("lat"), lax.axis_size("tm")
    my_tm, my_lat = lax.axis_index("tm"), lax.axis_index("lat")
    south = my_lat >= nlat // 2
    levels = ntm.bit_length() - 1
    bits_a = list(range(levels))
    bits_b = bits_a[-1:] + bits_a[:-1]

    pairs = owner_map.reshape(nlat, ntm, -1, 2)
    owned = pairs.shape[2]
    small, large = jnp.min(pairs, axis=3), jnp.max(pairs, axis=3)
    wanted = jnp.concatenate(
        [
            from_here(x.transpose(1, 0, 2), b, my_tm, my_lat)
            for x, b in ((small, bits_a), (large, bits_b))
        ]
    )
    wanted = table_column(wanted, order_count)
    place = (wanted[:, None] == jnp.arange(order_count, dtype=jnp.int32)[None, :]).astype(
        jnp.bfloat16
    )
    tables = [jnp.asarray(t) for t in longitude_tables(nlon, order_count)]
    time_mats = jnp.asarray(time_matrices(frame_count, ntm))
    where = jnp.stack([south.astype(jnp.int32), my_tm.astype(jnp.int32)])

    mine = lax.dynamic_slice(pairs, (my_lat, my_tm, 0, 0), (1, 1, owned, 2))[0, 0]
    mine = jnp.stack([jnp.min(mine, axis=1), jnp.max(mine, axis=1)])
    mine = jnp.pad(mine, ((0, 0), (0, GROUP - owned)), mode="edge")
    parity = jnp.broadcast_to(mine[:, :, None], (2, GROUP, 128))
    here = jnp.stack([my_lat.astype(jnp.int32), my_tm.astype(jnp.int32)])

    quarter = row_count // ROWS // 4
    parts = [(sum(QUARTERS[:i]) * quarter, n * quarter) for i, n in enumerate(QUARTERS)]
    pieces = []
    for part in parts:
        if pieces:
            where = after(where, pieces[-1][0])
        pieces.append(transform_chunk(part, where, frames, tables, time_mats, place))
    bands, early, waits = [], [], []
    for i, piece in enumerate(pieces):
        if i == len(pieces) - 1:
            made = [
                polynomials(after(mine[g], *waits), g, order_count, nlat, row_count, parts)
                for g in range(2)
            ]
            early = [token for _, token in made]
        band, sent = reduce_over_time(piece, bits_a, bits_b, nlat, early)
        waits = [sent, pieces[-1][0]]
        bands.append(band)
    lanes_at, acc = (0, 0), ()
    for i, (band, (_, blocks)) in enumerate(zip(bands, parts)):
        band = exchange(band, owned, range(nlat - 1, -1, -1))
        if acc:
            band = [after(band[0], *acc), *band[1:]]
        lanes = [(nlat // 2 - g * nlat // 4) * blocks * ROWS for g in range(2)]
        acc = contract_chunk(
            i == len(parts) - 1, here, band, parity, [m[0] for m in made], lanes_at, lanes,
            acc, (0, order_count // 2), ntm,
        )
        lanes_at = tuple(x + y for x, y in zip(lanes_at, lanes))
    sums = [acc[0]] + [swap_with(acc[d], "tm", d) for d in range(1, ntm)]
    return arrange(here, owner_map, sums, owned)


def solution(mesh):
    return jax.shard_map(
        shards,
        mesh=mesh,
        in_specs=(P("tm", "lat", None), P()),
        out_specs=P(None, "lat", None, "tm"),
        check_vma=False,
    )
```
